32 devices in a mesh: gx: 8 (over z, y), gy: 2 (over core), gz: 2 (over x).
Axes of the slice: x: 2, y: 2, z: 4, core: 2. Of those that a mesh axis runs over, the one named last changes fastest.
Arguments:
- velocity: float32 [3, 4, 64, 768], P(None, 'gz', 'gx', 'gy'), may hold values from -6 to 6
- adjoint: float32 [3, 4, 64, 768], P(None, 'gz', 'gx', 'gy'), may hold values from -0.3 to 0.3
- viscosity: float32 [4, 64, 768], P('gz', 'gx', 'gy'), may hold values from 0.5 to 5
- hang_flags: int32 [64, 256], P('gx', 'gy'), may hold values 0 or 1
- hang_index: int32 [64, 256], P('gx', 'gy'), may hold values from 0 to 7
- block_table: float32 [8, 3, 3], replicated, may hold values from -0.5 to 1
- friction: float32 [64, 768], P('gx', ('gy', 'gz')), may hold values from -3 to 3
- basal_mask: int32 [64, 768], P('gx', ('gy', 'gz')), may hold values 0 or 1
- direction: float32 [64, 768], P('gx', ('gy', 'gz')), may hold values from -6 to 6
Outputs:
- stokes_image: float32 [3, 4, 64, 768], P(None, 'gz', 'gx', 'gy')
- hessian_dir: float32 [64, 768], P('gx', ('gy', 'gz'))
The draws below stay inside these ranges and needn't reach their ends.
All inputs are finite; a program needn't handle non-finite values. No bound on the sum of `hang_flags` or of `basal_mask` on one device may be relied on, other than what follows from the above.
Results may differ from the reference program's by a relative error of at most 0.00025.
Values sent between devices are 32-bit elements; how exact they have to be, the bound alone decides.
A program may use at most 64 MiB of HBM per device.

```python
import math
import jax
import jax.numpy as jnp
from jax import lax

CY = 384
NB = 8
NX = 64
NY = 768
NZ = 4
N_GY = 2


def set_ends(drawn, own_key, low, largest):
    shape = drawn.shape
    spot = [jax.random.randint(jax.random.fold_in(own_key, axis), (), 0, shape[axis]) for axis in range(len(shape))]
    drawn = drawn.at[tuple(spot)].set(low)
    longest = shape.index(max(shape))
    spot[longest] = (spot[longest] + 1) % shape[longest]
    return drawn.at[tuple(spot)].set(largest)


def level_of(key, shape, cuts, least, largest):
    factor_of, own = 1.0, jax.random.fold_in(key, 6)
    for axis_at, shards_of in cuts:
        draws = jnp.exp(jax.random.uniform(jax.random.fold_in(own, axis_at), (shards_of,), jnp.float32, least / len(cuts), largest / len(cuts)))
        factor_of = factor_of * jnp.repeat(draws, shape[axis_at] // shards_of).reshape([-1 if axis == axis_at else 1 for axis in range(len(shape))])
    return factor_of


def gaussian(stream_key, extent, spread, most, pieces=(), kind=jnp.bfloat16):
    values = spread * jax.random.normal(stream_key, extent, jnp.float32)
    if pieces:
        values = values * level_of(stream_key, extent, pieces, -0.22, 0.18)
    return jnp.clip(values, -most, most).astype(kind)


def setup_inputs(seed: int = 0) -> dict:
    keys = jax.random.split(jax.random.key(seed), 10)
    return {
        "velocity": gaussian(keys[0], (3, NZ, NX, NY), 1.0, 6.0, ((1, 2), (2, 8), (3, 2)), jnp.float32),
        "adjoint": gaussian(keys[1], (3, NZ, NX, NY), 0.05, 0.3, ((1, 2), (2, 8), (3, 2)), jnp.float32),
        "viscosity": jnp.clip(jnp.exp(math.log(5.0) - 2.3025851 * jax.random.uniform(keys[2], (NZ, NX, NY), jnp.float32) ** level_of(keys[2], (NZ, NX, NY), ((0, 2), (1, 8), (2, 2)), -0.2, 0.2)), 0.5, 5.0),
        "hang_flags": set_ends((jax.random.randint(keys[3], (NX, NY // 3), 0, 4) < 1).astype(jnp.int32), jax.random.fold_in(keys[3], 1), 0, 1),
        "hang_index": set_ends(jax.random.randint(keys[4], (NX, NY // 3), 0, NB), jax.random.fold_in(keys[4], 1), 0, NB - 1).astype(jnp.int32),
        "block_table": jnp.clip(jax.random.uniform(keys[5], (NB, 3, 3), jnp.float32, -0.5, 1.0), -0.5, 1.0),
        "friction": gaussian(keys[6], (NX, NY), 0.5, 3.0, ((0, 8), (1, 4)), jnp.float32),
        "basal_mask": set_ends((jax.random.randint(keys[7], (NX, NY), 0, 4) < 3).astype(jnp.int32), jax.random.fold_in(keys[7], 1), 0, 1),
        "direction": gaussian(keys[8], (NX, NY), 1.0, 6.0, ((0, 8), (1, 4)), jnp.float32),
    }


reg_weight = 0.05


def block_matrices(hang_flags, hang_index, block_table):
    groups = CY // 3
    one_hot = (hang_index.reshape(NX, N_GY, groups)[..., None] == jnp.arange(NB, dtype=jnp.int32)).astype(jnp.float32)
    blocks = jnp.einsum('xhgn,nmk->mkxhg', one_hot, block_table.astype(jnp.float32), precision=lax.Precision.HIGHEST)
    hanging = hang_flags.reshape(NX, N_GY, groups).astype(jnp.float32)
    identity = jnp.eye(3, dtype=jnp.float32)[:, :, None, None, None]
    return hanging * blocks + (1.0 - hanging) * identity


def apply_blocks(local_blocks, field, transpose):
    groups = CY // 3
    levels = field.shape[1]
    shaped = field.reshape(3, levels, NX, N_GY, 3, groups)
    if transpose:
        mixed = jnp.einsum('mkxhg,czxhmg->czxhkg', local_blocks, shaped, precision=lax.Precision.HIGHEST)
    else:
        mixed = jnp.einsum('mkxhg,czxhkg->czxhmg', local_blocks, shaped, precision=lax.Precision.HIGHEST)
    return mixed.reshape(field.shape)


def shifted(padded, spatial, offset):
    lead = padded.ndim - 3
    index = [slice(None)] * lead + [slice(1, -1)] * 3
    if offset == 1:
        index[lead + spatial] = slice(2, None)
    elif offset == -1:
        index[lead + spatial] = slice(None, -2)
    return padded[tuple(index)]


def stencil(padded_vel, padded_visc):
    centre_vel = shifted(padded_vel, 0, 0)
    centre_visc = shifted(padded_visc, 0, 0)
    total = jnp.zeros(centre_vel.shape, jnp.float32)
    for spatial in range(3):
        for offset in (1, -1):
            face = 0.5 * (centre_visc + shifted(padded_visc, spatial, offset))
            total = total + face[None] * (centre_vel - shifted(padded_vel, spatial, offset))
    return total


def laplace(padded):
    return 4.0 * padded[1:-1, 1:-1] - padded[2:, 1:-1] - padded[:-2, 1:-1] - padded[1:-1, 2:] - padded[1:-1, :-2]


def reference(velocity, adjoint, viscosity, hang_flags, hang_index, block_table, friction, basal_mask, direction):
    local_blocks = block_matrices(hang_flags, hang_index, block_table)
    constrained = apply_blocks(local_blocks, velocity, False)
    padded_vel = jnp.pad(constrained, ((0, 0), (1, 1), (1, 1), (1, 1)))
    padded_visc = jnp.pad(viscosity, 1)
    applied = stencil(padded_vel, padded_visc)
    stokes_image = apply_blocks(local_blocks, applied, True)
    column_sums = jnp.sum(stokes_image * adjoint, axis=(0, 1))
    bilaplace = laplace(jnp.pad(laplace(jnp.pad(direction, 1)), 1))
    hessian_dir = reg_weight * bilaplace + basal_mask.astype(jnp.float32) * (jnp.exp(friction) * column_sums)
    return stokes_image, hessian_dir
```

```python
import functools

import jax
import jax.numpy as jnp
from jax import lax
from jax.experimental import pallas as pl
from jax.experimental.pallas import tpu as pltpu
from jax.sharding import PartitionSpec as P

NB = 8
REG = 0.05
MESH = pl.DeviceIdType.MESH
XU, XD, YL, YR, ZZ, CP, CC, PS = range(8)


def shift(value, by, axis):
    return pltpu.roll(value, by % value.shape[axis], axis)


def kernel(
    sizes,
    vel_h, adj_h, visc_h, flags_h, index_h, table, fric_h, mask_h, dir_h,
    out, hess,
    vel, adj, flags, index, fric, mask, direc,
    cons, xs_u, xs_d, xr_u, xr_d, zr, yr_l, yr_r, big, cs_p, cs_c, cr_p, cr_c, ps, pr,
    load_sem, send_sem, recv_sem,
):
    ngx, ngy, ngz = sizes
    gx, gy, gz = (lax.axis_index(axis) for axis in ("gx", "gy", "gz"))
    rows, cols = cons.shape[2], cons.shape[3]
    tiles = [slice(128 * m, 128 * (m + 1)) for m in range(3)]
    half = direc.shape[1]
    low = gz == 0
    has_u, has_d = gx > 0, gx < ngx - 1
    has_l, has_r = gy > 0, gy < ngy - 1
    has_c = jnp.where(low, gy, ngy - 1 - gy) > 0
    cross_gy = jnp.where(low, gy + ngy - 1, gy + 1) % ngy

    loads = [
        pltpu.make_async_copy(src, dst, load_sem.at[i])
        for i, (src, dst) in enumerate(
            (
                (vel_h, vel), (visc_h, cons.at[:, 3]), (flags_h, flags), (index_h, index),
                (dir_h, direc), (adj_h, adj), (fric_h, fric), (mask_h, mask),
            )
        )
    ]
    for load in loads:
        load.start()

    up = {"gx": (gx + ngx - 1) % ngx}
    down = {"gx": (gx + 1) % ngx}
    left = {"gy": (gy + ngy - 1) % ngy}
    right = {"gy": (gy + 1) % ngy}
    partner = {"gz": 1 - gz}
    cross = {"gy": cross_gy, "gz": 1 - gz}
    greet = ((has_u, up), (has_d, down), (has_l, left), (has_r, right), (has_c, cross))

    barrier = pltpu.get_barrier_semaphore()
    pl.semaphore_signal(barrier, inc=1, device_id=partner, device_id_type=MESH)
    for has, device in greet:
        @pl.when(has)
        def _():
            pl.semaphore_signal(barrier, inc=1, device_id=device, device_id_type=MESH)

    def remote(src, dst, at, device):
        return pltpu.make_async_remote_copy(
            src_ref=src, dst_ref=dst, send_sem=send_sem.at[at], recv_sem=recv_sem.at[at],
            device_id=device, device_id_type=MESH,
        )

    to_xu = remote(xs_d, xr_u, XU, down)
    to_xd = remote(xs_u, xr_d, XD, up)
    to_yl = remote(cons.at[:, :, :, cols - 128:], yr_l, YL, right)
    to_yr = remote(cons.at[:, :, :, :128], yr_r, YR, left)
    to_z = remote(cons.at[1 - gz], zr, ZZ, partner)
    to_cp = remote(cs_p, cr_p, CP, partner)
    to_cc = remote(cs_c, cr_c, CC, cross)
    to_ps = remote(ps, pr, PS, partner)

    for load in loads[:5]:
        load.wait()
    hanging = flags[...] == 1
    number = index[...]
    chosen = [number == n for n in range(NB)]
    block = [[None] * 3 for _ in range(3)]
    for m in range(3):
        for k in range(3):
            value = jnp.full(number.shape, table[m, k, 0], jnp.float32)
            for n in range(1, NB):
                value = jnp.where(chosen[n], table[m, k, n], value)
            block[m][k] = jnp.where(hanging, value, 1.0 if m == k else 0.0)
    for z in range(2):
        for c in range(3):
            slots = [vel[c, z, :, tile] for tile in tiles]
            for m in range(3):
                cons[z, c, :, tiles[m]] = (
                    block[m][0] * slots[0] + block[m][1] * slots[1] + block[m][2] * slots[2]
                )
    for z in range(2):
        for c in range(4):
            at = 4 * z + c
            xs_u[at:at + 1, :cols] = cons[z, c, 0:1, :]
            xs_d[at:at + 1, :cols] = cons[z, c, rows - 1:rows, :]
    for r in range(2):
        for send, row in ((xs_u, r), (xs_d, rows - 2 + r)):
            send[2 * r:2 * r + 1, cols:cols + 128] = direc[row:row + 1, :128]
            send[2 * r + 1:2 * r + 2, cols:cols + half - 128] = direc[row:row + 1, 128:]

    waits = sum((has.astype(jnp.int32) for has, _ in greet), jnp.int32(1))
    pl.semaphore_wait(barrier, waits)
    to_z.start()
    for has, copy in ((has_d, to_xu), (has_u, to_xd), (has_r, to_yl), (has_l, to_yr)):
        @pl.when(has)
        def _():
            copy.start()

    big[...] = jnp.zeros_like(big)
    for has, copy, buffer in ((has_u, to_xu, xr_u), (has_d, to_xd, xr_d)):
        @pl.when(has)
        def _():
            copy.wait_recv()

        @pl.when(jnp.logical_not(has))
        def _():
            buffer[...] = jnp.zeros_like(buffer)
    big[rows:2 * rows, 128:128 + half] = direc[...]
    for buffer, row in ((xr_u, rows - 2), (xr_d, 2 * rows)):
        for r in range(2):
            big[row + r:row + r + 1, 128:256] = buffer[2 * r:2 * r + 1, cols:cols + 128]
            big[row + r:row + r + 1, 256:128 + half] = (
                buffer[2 * r + 1:2 * r + 2, cols:cols + half - 128]
            )
    wide = big[...]
    edge_low, edge_high = wide[:, 128:256], wide[:, half:half + 128]
    cs_p[...] = jnp.where(low, edge_high, edge_low)
    cs_c[...] = jnp.where(low, edge_low, edge_high)
    to_cp.start()

    @pl.when(has_c)
    def _():
        to_cc.start()

    for has, copy, buffer in ((has_l, to_yl, yr_l), (has_r, to_yr, yr_r)):
        @pl.when(has)
        def _():
            copy.wait_recv()

        @pl.when(jnp.logical_not(has))
        def _():
            buffer[...] = jnp.zeros_like(buffer)
    to_z.wait_recv()
    for load in loads[5:]:
        load.wait()

    row_at = lax.broadcasted_iota(jnp.int32, (rows, cols), 0)
    own = [[cons[z, c] for c in range(4)] for z in range(2)]
    layer = [zr[c] for c in range(4)]
    below = [jnp.where(low, 0.0, a) for a in layer]
    above = [jnp.where(low, a, 0.0) for a in layer]
    stack = [below, own[0], own[1], above]
    total = [[None] * 3 for _ in range(2)]
    z_visc = [stack[i][3] + stack[i + 1][3] for i in range(3)]
    for c in range(3):
        flux = [z_visc[i] * (stack[i + 1][c] - stack[i][c]) for i in range(3)]
        for z in range(2):
            total[z][c] = flux[z] - flux[z + 1]
    for z in range(2):
        up_of, down_of, ext, ext_next = [], [], [], []
        for c in range(4):
            at = 4 * z + c
            a = own[z][c]
            up_of.append(jnp.where(row_at == 0, xr_u[at:at + 1, :cols], shift(a, 1, 0)))
            down_of.append(jnp.where(row_at == rows - 1, xr_d[at:at + 1, :cols], shift(a, -1, 0)))
            wide_a = jnp.concatenate([yr_l[z, c], a, yr_r[z, c]], axis=1)
            ext.append(wide_a)
            ext_next.append(shift(wide_a, -1, 1))
        visc_u, visc_d = own[z][3] + up_of[3], own[z][3] + down_of[3]
        visc_y = ext[3] + ext_next[3]
        for c in range(3):
            a = own[z][c]
            flux = visc_y * (ext[c] - ext_next[c])
            total[z][c] = 0.5 * (
                total[z][c]
                + visc_u * (a - up_of[c])
                + visc_d * (a - down_of[c])
                + (flux - shift(flux, 1, 1))[:, 128:128 + cols]
            )
    sums = [None] * 3
    for z in range(2):
        for c in range(3):
            for k in range(3):
                image = (
                    block[0][k] * total[z][c][:, tiles[0]]
                    + block[1][k] * total[z][c][:, tiles[1]]
                    + block[2][k] * total[z][c][:, tiles[2]]
                )
                out[c, z, :, tiles[k]] = image
                term = image * adj[c, z, :, tiles[k]]
                sums[k] = term if sums[k] is None else sums[k] + term
    sums = jnp.concatenate(sums, axis=1)
    first, second = sums[:, :half], sums[:, half:]
    ps[...] = jnp.where(low, second, first)
    to_ps.start()
    mine = jnp.where(low, first, second)

    to_cp.wait_recv()

    @pl.when(has_c)
    def _():
        to_cc.wait_recv()

    @pl.when(jnp.logical_not(has_c))
    def _():
        cr_c[...] = jnp.zeros_like(cr_c)

    from_p, from_c = cr_p[...], cr_c[...]
    from_low = jnp.where(low, from_c, from_p)
    from_high = shift(jnp.where(low, from_p, from_c), half % 128, 1)
    lane = lax.broadcasted_iota(jnp.int32, from_low.shape, 1)
    wide = jnp.concatenate(
        [from_low, wide[:, 128:256], jnp.where(lane < half % 128, wide[:, 256:], from_high)], axis=1
    )

    def laplace(v):
        return 4.0 * v - shift(v, 1, 0) - shift(v, -1, 0) - shift(v, 1, 1) - shift(v, -1, 1)

    row_g = gx * rows - rows + lax.broadcasted_iota(jnp.int32, wide.shape, 0)
    col_g = (gy * ngz + gz) * half - 128 + lax.broadcasted_iota(jnp.int32, wide.shape, 1)
    inside = (row_g >= 0) & (row_g < ngx * rows) & (col_g >= 0) & (col_g < ngy * ngz * half)
    twice = laplace(jnp.where(inside, laplace(wide), 0.0))[rows:2 * rows, 128:128 + half]
    scale = mask[...].astype(jnp.float32) * jnp.exp(fric[...])

    to_ps.wait_recv()
    hess[...] = REG * twice + scale * (mine + pr[...])

    for copy in (to_z, to_cp, to_ps):
        copy.wait_send()
    for has, copy in (
        (has_d, to_xu), (has_u, to_xd), (has_r, to_yl), (has_l, to_yr), (has_c, to_cc)
    ):
        @pl.when(has)
        def _():
            copy.wait_send()


def local(sizes, velocity, adjoint, viscosity, hang_flags, hang_index, block_table, friction, basal_mask, direction):
    _, levels, rows, cols = velocity.shape
    assert levels == 2 and sizes[2] == 2 and cols == 384
    half = direction.shape[1]
    f32 = jnp.float32
    vmem = pltpu.VMEM
    anywhere = pl.BlockSpec(memory_space=pl.ANY)
    return pl.pallas_call(
        functools.partial(kernel, sizes),
        out_shape=(
            jax.ShapeDtypeStruct(velocity.shape, f32),
            jax.ShapeDtypeStruct(direction.shape, f32),
        ),
        in_specs=[anywhere] * 5 + [pl.BlockSpec(memory_space=pltpu.SMEM)] + [anywhere] * 3,
        out_specs=(pl.BlockSpec(memory_space=vmem),) * 2,
        scratch_shapes=[
            vmem(velocity.shape, f32),
            vmem(velocity.shape, f32),
            vmem(hang_flags.shape, jnp.int32),
            vmem(hang_index.shape, jnp.int32),
            vmem(direction.shape, f32),
            vmem(direction.shape, jnp.int32),
            vmem(direction.shape, f32),
            vmem((levels, 4, rows, cols), f32),
            vmem((8, cols + 128), f32),
            vmem((8, cols + 128), f32),
            vmem((8, cols + 128), f32),
            vmem((8, cols + 128), f32),
            vmem((4, rows, cols), f32),
            vmem((levels, 4, rows, 128), f32),
            vmem((levels, 4, rows, 128), f32),
            vmem((3 * rows, 384), f32),
            vmem((3 * rows, 128), f32),
            vmem((3 * rows, 128), f32),
            vmem((3 * rows, 128), f32),
            vmem((3 * rows, 128), f32),
            vmem(direction.shape, f32),
            vmem(direction.shape, f32),
            pltpu.SemaphoreType.DMA((8,)),
            pltpu.SemaphoreType.DMA((8,)),
            pltpu.SemaphoreType.DMA((8,)),
        ],
        compiler_params=pltpu.CompilerParams(collective_id=0, has_side_effects=True),
        cost_estimate=pl.CostEstimate(flops=200_000, bytes_accessed=400_000, transcendentals=1536),
        name="hessian_apply",
    )(velocity, adjoint, viscosity, hang_flags, hang_index, jnp.transpose(block_table, (1, 2, 0)), friction, basal_mask, direction)


def solution(mesh):
    sizes = tuple(mesh.shape[axis] for axis in ("gx", "gy", "gz"))
    return jax.shard_map(
        functools.partial(local, sizes),
        mesh=mesh,
        in_specs=(
            P(None, "gz", "gx", "gy"),
            P(None, "gz", "gx", "gy"),
            P("gz", "gx", "gy"),
            P("gx", "gy"),
            P("gx", "gy"),
            P(),
            P("gx", ("gy", "gz")),
            P("gx", ("gy", "gz")),
            P("gx", ("gy", "gz")),
        ),
        out_specs=(P(None, "gz", "gx", "gy"), P("gx", ("gy", "gz"))),
        check_vma=False,
    )
```

```python
import functools

import jax
import jax.numpy as jnp
from jax import lax
from jax.experimental import pallas as pl
from jax.experimental.pallas import tpu as pltpu
from jax.sharding import PartitionSpec as P

NB = 8
REG = 0.05
LIMIT = 4 * 1024 * 1024
MESH = pl.DeviceIdType.MESH
XU, XD, YL, YR, ZZ, CP, CC, PS = range(8)


def shift(value, by, axis):
    return pltpu.roll(value, by % value.shape[axis], axis)


def kernel(
    sizes,
    vel_h, adj_h, visc_h, flags_h, index_h, table_h, fric_h, mask_h, dir_h,
    out, hess,
    table, vel, adj, flags, index, fric, mask, direc,
    cons, xs_u, xs_d, xr_u, xr_d, zr, yr_l, yr_r, big, cs_p, cs_c, cr_p, cr_c, ps, pr,
    load_sem, send_sem, recv_sem,
):
    ngx, ngy, ngz = sizes
    gx, gy, gz = (lax.axis_index(axis) for axis in ("gx", "gy", "gz"))
    rows, cols = cons.shape[2], cons.shape[3]
    tiles = [slice(128 * m, 128 * (m + 1)) for m in range(3)]
    half = direc.shape[1]
    low = gz == 0
    has_u, has_d = gx > 0, gx < ngx - 1
    has_l, has_r = gy > 0, gy < ngy - 1
    has_c = jnp.where(low, gy, ngy - 1 - gy) > 0
    cross_gy = jnp.where(low, gy + ngy - 1, gy + 1) % ngy

    loads = [
        pltpu.make_async_copy(src, dst, load_sem.at[i])
        for i, (src, dst) in enumerate(
            (
                (table_h, table), (flags_h, flags), (index_h, index), (vel_h, vel), (visc_h, cons.at[:, 3]),
                (dir_h, direc), (adj_h, adj), (fric_h, fric), (mask_h, mask),
            )
        )
    ]
    for load in loads:
        load.start()

    up = {"gx": (gx + ngx - 1) % ngx}
    down = {"gx": (gx + 1) % ngx}
    left = {"gy": (gy + ngy - 1) % ngy}
    right = {"gy": (gy + 1) % ngy}
    partner = {"gz": 1 - gz}
    cross = {"gy": cross_gy, "gz": 1 - gz}
    greet = ((has_u, up), (has_d, down), (has_l, left), (has_r, right), (has_c, cross))

    barrier = pltpu.get_barrier_semaphore()
    pl.semaphore_signal(barrier, inc=1, device_id=partner, device_id_type=MESH)
    for has, device in greet:
        @pl.when(has)
        def _():
            pl.semaphore_signal(barrier, inc=1, device_id=device, device_id_type=MESH)

    def remote(src, dst, at, device):
        return pltpu.make_async_remote_copy(
            src_ref=src, dst_ref=dst, send_sem=send_sem.at[at], recv_sem=recv_sem.at[at],
            device_id=device, device_id_type=MESH,
        )

    to_xu = remote(xs_d, xr_u, XU, down)
    to_xd = remote(xs_u, xr_d, XD, up)
    to_yl = remote(cons.at[:, :, :, cols - 128:], yr_l, YL, right)
    to_yr = remote(cons.at[:, :, :, :128], yr_r, YR, left)
    to_z = remote(cons.at[1 - gz], zr, ZZ, partner)
    to_cp = remote(cs_p, cr_p, CP, partner)
    to_cc = remote(cs_c, cr_c, CC, cross)
    to_ps = remote(ps, pr, PS, partner)

    for load in loads[:6]:
        load.wait()
    hanging = flags[...] == 1
    number = index[...]
    chosen = [number == n for n in range(NB)]
    block = [[None] * 3 for _ in range(3)]
    for m in range(3):
        for k in range(3):
            value = jnp.full(number.shape, table[m, k, 0], jnp.float32)
            for n in range(1, NB):
                value = jnp.where(chosen[n], table[m, k, n], value)
            block[m][k] = jnp.where(hanging, value, 1.0 if m == k else 0.0)
    for z in range(2):
        for c in range(3):
            slots = [vel[c, z, :, tile] for tile in tiles]
            for m in range(3):
                cons[z, c, :, tiles[m]] = (
                    block[m][0] * slots[0] + block[m][1] * slots[1] + block[m][2] * slots[2]
                )
    for z in range(2):
        for c in range(4):
            at = 4 * z + c
            xs_u[at:at + 1, :cols] = cons[z, c, 0:1, :]
            xs_d[at:at + 1, :cols] = cons[z, c, rows - 1:rows, :]
    for r in range(2):
        for send, row in ((xs_u, r), (xs_d, rows - 2 + r)):
            send[2 * r:2 * r + 1, cols:cols + 128] = direc[row:row + 1, :128]
            send[2 * r + 1:2 * r + 2, cols:cols + half - 128] = direc[row:row + 1, 128:]

    waits = sum((has.astype(jnp.int32) for has, _ in greet), jnp.int32(1))
    pl.semaphore_wait(barrier, waits)
    to_z.start()
    for has, copy in ((has_d, to_xu), (has_u, to_xd), (has_r, to_yl), (has_l, to_yr)):
        @pl.when(has)
        def _():
            copy.start()

    big[...] = jnp.zeros_like(big)
    for has, copy, buffer in ((has_u, to_xu, xr_u), (has_d, to_xd, xr_d)):
        @pl.when(has)
        def _():
            copy.wait_recv()

        @pl.when(jnp.logical_not(has))
        def _():
            buffer[...] = jnp.zeros_like(buffer)
    big[rows:2 * rows, 128:128 + half] = direc[...]
    for buffer, row in ((xr_u, rows - 2), (xr_d, 2 * rows)):
        for r in range(2):
            big[row + r:row + r + 1, 128:256] = buffer[2 * r:2 * r + 1, cols:cols + 128]
            big[row + r:row + r + 1, 256:128 + half] = (
                buffer[2 * r + 1:2 * r + 2, cols:cols + half - 128]
            )
    wide = big[...]
    edge_low, edge_high = wide[:, 128:256], wide[:, half:half + 128]
    cs_p[...] = jnp.where(low, edge_high, edge_low)
    cs_c[...] = jnp.where(low, edge_low, edge_high)
    to_cp.start()

    @pl.when(has_c)
    def _():
        to_cc.start()

    for has, copy, buffer in ((has_l, to_yl, yr_l), (has_r, to_yr, yr_r)):
        @pl.when(has)
        def _():
            copy.wait_recv()

        @pl.when(jnp.logical_not(has))
        def _():
            buffer[...] = jnp.zeros_like(buffer)
    to_z.wait_recv()
    for load in loads[6:]:
        load.wait()

    row_at = lax.broadcasted_iota(jnp.int32, (rows, cols), 0)
    own = [[cons[z, c] for c in range(4)] for z in range(2)]
    layer = [zr[c] for c in range(4)]
    below = [jnp.where(low, 0.0, a) for a in layer]
    above = [jnp.where(low, a, 0.0) for a in layer]
    stack = [below, own[0], own[1], above]
    total = [[None] * 3 for _ in range(2)]
    z_visc = [stack[i][3] + stack[i + 1][3] for i in range(3)]
    for c in range(3):
        flux = [z_visc[i] * (stack[i + 1][c] - stack[i][c]) for i in range(3)]
        for z in range(2):
            total[z][c] = flux[z] - flux[z + 1]
    for z in range(2):
        up_of, down_of, ext, ext_next = [], [], [], []
        for c in range(4):
            at = 4 * z + c
            a = own[z][c]
            up_of.append(jnp.where(row_at == 0, xr_u[at:at + 1, :cols], shift(a, 1, 0)))
            down_of.append(jnp.where(row_at == rows - 1, xr_d[at:at + 1, :cols], shift(a, -1, 0)))
            wide_a = jnp.concatenate([yr_l[z, c], a, yr_r[z, c]], axis=1)
            ext.append(wide_a)
            ext_next.append(shift(wide_a, -1, 1))
        visc_u, visc_d = own[z][3] + up_of[3], own[z][3] + down_of[3]
        visc_y = ext[3] + ext_next[3]
        for c in range(3):
            a = own[z][c]
            flux = visc_y * (ext[c] - ext_next[c])
            total[z][c] = 0.5 * (
                total[z][c]
                + visc_u * (a - up_of[c])
                + visc_d * (a - down_of[c])
                + (flux - shift(flux, 1, 1))[:, 128:128 + cols]
            )
    sums = [None] * 3
    for z in range(2):
        for c in range(3):
            for k in range(3):
                image = (
                    block[0][k] * total[z][c][:, tiles[0]]
                    + block[1][k] * total[z][c][:, tiles[1]]
                    + block[2][k] * total[z][c][:, tiles[2]]
                )
                out[c, z, :, tiles[k]] = image
                term = image * adj[c, z, :, tiles[k]]
                sums[k] = term if sums[k] is None else sums[k] + term
    sums = jnp.concatenate(sums, axis=1)
    first, second = sums[:, :half], sums[:, half:]
    ps[...] = jnp.where(low, second, first)
    to_ps.start()
    mine = jnp.where(low, first, second)

    to_cp.wait_recv()

    @pl.when(has_c)
    def _():
        to_cc.wait_recv()

    @pl.when(jnp.logical_not(has_c))
    def _():
        cr_c[...] = jnp.zeros_like(cr_c)

    from_p, from_c = cr_p[...], cr_c[...]
    from_low = jnp.where(low, from_c, from_p)
    from_high = shift(jnp.where(low, from_p, from_c), half % 128, 1)
    lane = lax.broadcasted_iota(jnp.int32, from_low.shape, 1)
    wide = jnp.concatenate(
        [from_low, wide[:, 128:256], jnp.where(lane < half % 128, wide[:, 256:], from_high)], axis=1
    )

    def laplace(v):
        return 4.0 * v - shift(v, 1, 0) - shift(v, -1, 0) - shift(v, 1, 1) - shift(v, -1, 1)

    row_g = gx * rows - rows + lax.broadcasted_iota(jnp.int32, wide.shape, 0)
    col_g = (gy * ngz + gz) * half - 128 + lax.broadcasted_iota(jnp.int32, wide.shape, 1)
    inside = (row_g >= 0) & (row_g < ngx * rows) & (col_g >= 0) & (col_g < ngy * ngz * half)
    twice = laplace(jnp.where(inside, laplace(wide), 0.0))[rows:2 * rows, 128:128 + half]
    scale = mask[...].astype(jnp.float32) * jnp.exp(fric[...])

    to_ps.wait_recv()
    hess[...] = REG * twice + scale * (mine + pr[...])

    for copy in (to_z, to_cp, to_ps):
        copy.wait_send()
    for has, copy in (
        (has_d, to_xu), (has_u, to_xd), (has_r, to_yl), (has_l, to_yr), (has_c, to_cc)
    ):
        @pl.when(has)
        def _():
            copy.wait_send()


def store(image_v, hess_v, image_h, hess_h, sem):
    copies = [
        pltpu.make_async_copy(image_v, image_h, sem.at[0]),
        pltpu.make_async_copy(hess_v, hess_h, sem.at[1]),
    ]
    for copy in copies:
        copy.start()
    for copy in copies:
        copy.wait()


def local(sizes, velocity, adjoint, viscosity, hang_flags, hang_index, block_table, friction, basal_mask, direction):
    _, levels, rows, cols = velocity.shape
    assert levels == 2 and sizes[2] == 2 and cols == 384
    half = direction.shape[1]
    f32 = jnp.float32
    vmem = pltpu.VMEM
    anywhere = pl.BlockSpec(memory_space=pltpu.HBM)
    arguments = [
        pltpu.with_memory_space_constraint(array, pltpu.HBM)
        for array in (
            velocity, adjoint, viscosity, hang_flags, hang_index,
            jnp.transpose(block_table, (1, 2, 0)), friction, basal_mask, direction,
        )
    ]
    image, hess = pl.pallas_call(
        functools.partial(kernel, sizes),
        out_shape=(vmem(velocity.shape, f32), vmem(direction.shape, f32)),
        in_specs=[anywhere] * 9,
        out_specs=(pl.BlockSpec(memory_space=vmem),) * 2,
        scratch_shapes=[
            pltpu.SMEM((3, 3, NB), f32),
            vmem(velocity.shape, f32),
            vmem(velocity.shape, f32),
            vmem(hang_flags.shape, jnp.int32),
            vmem(hang_index.shape, jnp.int32),
            vmem(direction.shape, f32),
            vmem(direction.shape, jnp.int32),
            vmem(direction.shape, f32),
            vmem((levels, 4, rows, cols), f32),
            vmem((8, cols + 128), f32),
            vmem((8, cols + 128), f32),
            vmem((8, cols + 128), f32),
            vmem((8, cols + 128), f32),
            vmem((4, rows, cols), f32),
            vmem((levels, 4, rows, 128), f32),
            vmem((levels, 4, rows, 128), f32),
            vmem((3 * rows, 384), f32),
            vmem((3 * rows, 128), f32),
            vmem((3 * rows, 128), f32),
            vmem((3 * rows, 128), f32),
            vmem((3 * rows, 128), f32),
            vmem(direction.shape, f32),
            vmem(direction.shape, f32),
            pltpu.SemaphoreType.DMA((9,)),
            pltpu.SemaphoreType.DMA((8,)),
            pltpu.SemaphoreType.DMA((8,)),
        ],
        compiler_params=pltpu.CompilerParams(collective_id=0, has_side_effects=True, vmem_limit_bytes=LIMIT),
        cost_estimate=pl.CostEstimate(flops=200_000, bytes_accessed=400_000, transcendentals=1536),
        name="hessian_apply",
    )(*arguments)
    return pl.pallas_call(
        store,
        out_shape=(
            jax.ShapeDtypeStruct(velocity.shape, f32),
            jax.ShapeDtypeStruct(direction.shape, f32),
        ),
        in_specs=[pl.BlockSpec(memory_space=vmem)] * 2,
        out_specs=(anywhere,) * 2,
        scratch_shapes=[pltpu.SemaphoreType.DMA((2,))],
        compiler_params=pltpu.CompilerParams(vmem_limit_bytes=LIMIT),
        name="store",
    )(image, hess)


def solution(mesh):
    sizes = tuple(mesh.shape[axis] for axis in ("gx", "gy", "gz"))
    return jax.shard_map(
        functools.partial(local, sizes),
        mesh=mesh,
        in_specs=(
            P(None, "gz", "gx", "gy"),
            P(None, "gz", "gx", "gy"),
            P("gz", "gx", "gy"),
            P("gx", "gy"),
            P("gx", "gy"),
            P(),
            P("gx", ("gy", "gz")),
            P("gx", ("gy", "gz")),
            P("gx", ("gy", "gz")),
        ),
        out_specs=(P(None, "gz", "gx", "gy"), P("gx", ("gy", "gz"))),
        check_vma=False,
    )
```

```python
import functools

import jax
import jax.numpy as jnp
from jax import lax
from jax.experimental import pallas as pl
from jax.experimental.pallas import tpu as pltpu
from jax.sharding import PartitionSpec as P

NB = 8
REG = 0.05
LIMIT = 4 * 1024 * 1024
MESH = pl.DeviceIdType.MESH
XU, XD, YL, YR, ZZ, ZV, CP, CC, PS = range(9)


def shift(value, by, axis):
    return pltpu.roll(value, by % value.shape[axis], axis)


def kernel(
    sizes,
    vel_h, adj_h, visc_h, flags_h, index_h, table_h, fric_h, mask_h, dir_h,
    out, hess,
    table, vel, adj, flags, index, fric, mask, direc,
    cons, xs_u, xs_d, xr_u, xr_d, zr, yr_l, yr_r, big, cs_p, cs_c, cr_p, cr_c, ps, pr,
    load_sem, send_sem, recv_sem,
):
    ngx, ngy, ngz = sizes
    gx, gy, gz = (lax.axis_index(axis) for axis in ("gx", "gy", "gz"))
    rows, cols = cons.shape[2], cons.shape[3]
    tiles = [slice(128 * m, 128 * (m + 1)) for m in range(3)]
    half = direc.shape[1]
    low = gz == 0
    has_u, has_d = gx > 0, gx < ngx - 1
    has_l, has_r = gy > 0, gy < ngy - 1
    has_c = jnp.where(low, gy, ngy - 1 - gy) > 0
    cross_gy = jnp.where(low, gy + ngy - 1, gy + 1) % ngy

    loads = [
        pltpu.make_async_copy(src, dst, load_sem.at[i])
        for i, (src, dst) in enumerate(
            (
                (table_h, table), (flags_h, flags), (index_h, index), (vel_h, vel), (visc_h, cons.at[:, 3]),
                (dir_h, direc), (adj_h, adj), (fric_h, fric), (mask_h, mask),
            )
        )
    ]
    for load in loads:
        load.start()

    up = {"gx": (gx + ngx - 1) % ngx}
    down = {"gx": (gx + 1) % ngx}
    left = {"gy": (gy + ngy - 1) % ngy}
    right = {"gy": (gy + 1) % ngy}
    partner = {"gz": 1 - gz}
    cross = {"gy": cross_gy, "gz": 1 - gz}
    greet = ((has_u, up), (has_d, down), (has_l, left), (has_r, right), (has_c, cross))

    barrier = pltpu.get_barrier_semaphore()
    pl.semaphore_signal(barrier, inc=1, device_id=partner, device_id_type=MESH)
    for has, device in greet:
        @pl.when(has)
        def _():
            pl.semaphore_signal(barrier, inc=1, device_id=device, device_id_type=MESH)

    def remote(src, dst, at, device):
        return pltpu.make_async_remote_copy(
            src_ref=src, dst_ref=dst, send_sem=send_sem.at[at], recv_sem=recv_sem.at[at],
            device_id=device, device_id_type=MESH,
        )

    to_xu = remote(xs_d, xr_u, XU, down)
    to_xd = remote(xs_u, xr_d, XD, up)
    to_yl = remote(cons.at[:, :, :, cols - 128:], yr_l, YL, right)
    to_yr = remote(cons.at[:, :, :, :128], yr_r, YR, left)
    near, far = 1 - gz, gz
    to_z = remote(vel_h.at[:, near], zr.at[:3], ZZ, partner)
    to_zv = remote(visc_h.at[near], zr.at[3], ZV, partner)
    to_cp = remote(cs_p, cr_p, CP, partner)
    to_cc = remote(cs_c, cr_c, CC, cross)
    to_ps = remote(ps, pr, PS, partner)

    waits = sum((has.astype(jnp.int32) for has, _ in greet), jnp.int32(1))
    pl.semaphore_wait(barrier, waits)
    to_z.start()
    to_zv.start()

    for load in loads[:6]:
        load.wait()
    hanging = flags[...] == 1
    number = index[...]
    chosen = [number == n for n in range(NB)]
    block = [[None] * 3 for _ in range(3)]
    for m in range(3):
        for k in range(3):
            value = jnp.full(number.shape, table[m, k, 0], jnp.float32)
            for n in range(1, NB):
                value = jnp.where(chosen[n], table[m, k, n], value)
            block[m][k] = jnp.where(hanging, value, 1.0 if m == k else 0.0)
    for z in range(2):
        for c in range(3):
            slots = [vel[c, z, :, tile] for tile in tiles]
            for m in range(3):
                cons[z, c, :, tiles[m]] = (
                    block[m][0] * slots[0] + block[m][1] * slots[1] + block[m][2] * slots[2]
                )
    for i, z in enumerate((near, far)):
        for c in range(4):
            at = 4 * i + c
            xs_u[at:at + 1, :cols] = cons[z, c, 0:1, :]
            xs_d[at:at + 1, :cols] = cons[z, c, rows - 1:rows, :]
    for r in range(2):
        for send, row in ((xs_u, r), (xs_d, rows - 2 + r)):
            send[2 * r:2 * r + 1, cols:cols + 128] = direc[row:row + 1, :128]
            send[2 * r + 1:2 * r + 2, cols:cols + half - 128] = direc[row:row + 1, 128:]

    for has, copy in ((has_d, to_xu), (has_u, to_xd), (has_r, to_yl), (has_l, to_yr)):
        @pl.when(has)
        def _():
            copy.start()

    big[...] = jnp.zeros_like(big)
    for has, copy, buffer in ((has_u, to_xu, xr_u), (has_d, to_xd, xr_d)):
        @pl.when(has)
        def _():
            copy.wait_recv()

        @pl.when(jnp.logical_not(has))
        def _():
            buffer[...] = jnp.zeros_like(buffer)
    big[rows:2 * rows, 128:128 + half] = direc[...]
    for buffer, row in ((xr_u, rows - 2), (xr_d, 2 * rows)):
        for r in range(2):
            big[row + r:row + r + 1, 128:256] = buffer[2 * r:2 * r + 1, cols:cols + 128]
            big[row + r:row + r + 1, 256:128 + half] = (
                buffer[2 * r + 1:2 * r + 2, cols:cols + half - 128]
            )
    wide = big[...]
    edge_low, edge_high = wide[:, 128:256], wide[:, half:half + 128]
    cs_p[...] = jnp.where(low, edge_high, edge_low)
    cs_c[...] = jnp.where(low, edge_low, edge_high)
    to_cp.start()

    @pl.when(has_c)
    def _():
        to_cc.start()

    for has, copy, buffer in ((has_l, to_yl, yr_l), (has_r, to_yr, yr_r)):
        @pl.when(has)
        def _():
            copy.wait_recv()

        @pl.when(jnp.logical_not(has))
        def _():
            buffer[...] = jnp.zeros_like(buffer)
    row_at = lax.broadcasted_iota(jnp.int32, (rows, cols), 0)
    own = [[cons[z, c] for c in range(4)] for z in (near, far)]
    total = [[None] * 3 for _ in range(2)]
    visc_z = own[0][3] + own[1][3]
    for c in range(3):
        flux = visc_z * (own[0][c] - own[1][c])
        total[0][c] = flux
        total[1][c] = own[1][3] * own[1][c] - flux
    for i, z in enumerate((near, far)):
        up_of, down_of, ext, ext_next = [], [], [], []
        for c in range(4):
            at = 4 * i + c
            a = own[i][c]
            up_of.append(jnp.where(row_at == 0, xr_u[at:at + 1, :cols], shift(a, 1, 0)))
            down_of.append(jnp.where(row_at == rows - 1, xr_d[at:at + 1, :cols], shift(a, -1, 0)))
            wide_a = jnp.concatenate([yr_l[z, c], a, yr_r[z, c]], axis=1)
            ext.append(wide_a)
            ext_next.append(shift(wide_a, -1, 1))
        visc_u, visc_d = own[i][3] + up_of[3], own[i][3] + down_of[3]
        visc_y = ext[3] + ext_next[3]
        for c in range(3):
            a = own[i][c]
            flux = visc_y * (ext[c] - ext_next[c])
            total[i][c] = (
                total[i][c]
                + visc_u * (a - up_of[c])
                + visc_d * (a - down_of[c])
                + (flux - shift(flux, 1, 1))[:, 128:128 + cols]
            )

    for load in loads[6:]:
        load.wait()
    sums = [None] * 3

    def finish(applied, c, z):
        applied = 0.5 * applied
        for k in range(3):
            image = (
                block[0][k] * applied[:, tiles[0]]
                + block[1][k] * applied[:, tiles[1]]
                + block[2][k] * applied[:, tiles[2]]
            )
            out[c, z, :, tiles[k]] = image
            term = image * adj[c, z, :, tiles[k]]
            sums[k] = term if sums[k] is None else sums[k] + term

    for c in range(3):
        finish(total[1][c], c, far)
    to_zv.wait_recv()
    visc_z = own[0][3] + zr[3]
    to_z.wait_recv()
    for c in range(3):
        slots = [zr[c, :, tile] for tile in tiles]
        layer = jnp.concatenate(
            [
                block[m][0] * slots[0] + block[m][1] * slots[1] + block[m][2] * slots[2]
                for m in range(3)
            ],
            axis=1,
        )
        finish(total[0][c] + visc_z * (own[0][c] - layer), c, near)
    sums = jnp.concatenate(sums, axis=1)
    first, second = sums[:, :half], sums[:, half:]
    ps[...] = jnp.where(low, second, first)
    to_ps.start()
    mine = jnp.where(low, first, second)

    to_cp.wait_recv()

    @pl.when(has_c)
    def _():
        to_cc.wait_recv()

    @pl.when(jnp.logical_not(has_c))
    def _():
        cr_c[...] = jnp.zeros_like(cr_c)

    from_p, from_c = cr_p[...], cr_c[...]
    from_low = jnp.where(low, from_c, from_p)
    from_high = shift(jnp.where(low, from_p, from_c), half % 128, 1)
    lane = lax.broadcasted_iota(jnp.int32, from_low.shape, 1)
    wide = jnp.concatenate(
        [from_low, wide[:, 128:256], jnp.where(lane < half % 128, wide[:, 256:], from_high)], axis=1
    )

    def laplace(v):
        return 4.0 * v - shift(v, 1, 0) - shift(v, -1, 0) - shift(v, 1, 1) - shift(v, -1, 1)

    row_g = gx * rows - rows + lax.broadcasted_iota(jnp.int32, wide.shape, 0)
    col_g = (gy * ngz + gz) * half - 128 + lax.broadcasted_iota(jnp.int32, wide.shape, 1)
    inside = (row_g >= 0) & (row_g < ngx * rows) & (col_g >= 0) & (col_g < ngy * ngz * half)
    twice = laplace(jnp.where(inside, laplace(wide), 0.0))[rows:2 * rows, 128:128 + half]
    scale = mask[...].astype(jnp.float32) * jnp.exp(fric[...])

    to_ps.wait_recv()
    hess[...] = REG * twice + scale * (mine + pr[...])

    for copy in (to_z, to_zv, to_cp, to_ps):
        copy.wait_send()
    for has, copy in (
        (has_d, to_xu), (has_u, to_xd), (has_r, to_yl), (has_l, to_yr), (has_c, to_cc)
    ):
        @pl.when(has)
        def _():
            copy.wait_send()


def store(image_v, hess_v, image_h, hess_h, sem):
    copies = [
        pltpu.make_async_copy(image_v, image_h, sem.at[0]),
        pltpu.make_async_copy(hess_v, hess_h, sem.at[1]),
    ]
    for copy in copies:
        copy.start()
    for copy in copies:
        copy.wait()


def local(sizes, velocity, adjoint, viscosity, hang_flags, hang_index, block_table, friction, basal_mask, direction):
    _, levels, rows, cols = velocity.shape
    assert levels == 2 and sizes[2] == 2 and cols == 384
    half = direction.shape[1]
    f32 = jnp.float32
    vmem = pltpu.VMEM
    anywhere = pl.BlockSpec(memory_space=pltpu.HBM)
    arguments = [
        pltpu.with_memory_space_constraint(array, pltpu.HBM)
        for array in (
            velocity, adjoint, viscosity, hang_flags, hang_index,
            jnp.transpose(block_table, (1, 2, 0)), friction, basal_mask, direction,
        )
    ]
    image, hess = pl.pallas_call(
        functools.partial(kernel, sizes),
        out_shape=(vmem(velocity.shape, f32), vmem(direction.shape, f32)),
        in_specs=[anywhere] * 9,
        out_specs=(pl.BlockSpec(memory_space=vmem),) * 2,
        scratch_shapes=[
            pltpu.SMEM((3, 3, NB), f32),
            vmem(velocity.shape, f32),
            vmem(velocity.shape, f32),
            vmem(hang_flags.shape, jnp.int32),
            vmem(hang_index.shape, jnp.int32),
            vmem(direction.shape, f32),
            vmem(direction.shape, jnp.int32),
            vmem(direction.shape, f32),
            vmem((levels, 4, rows, cols), f32),
            vmem((8, cols + 128), f32),
            vmem((8, cols + 128), f32),
            vmem((8, cols + 128), f32),
            vmem((8, cols + 128), f32),
            vmem((4, rows, cols), f32),
            vmem((levels, 4, rows, 128), f32),
            vmem((levels, 4, rows, 128), f32),
            vmem((3 * rows, 384), f32),
            vmem((3 * rows, 128), f32),
            vmem((3 * rows, 128), f32),
            vmem((3 * rows, 128), f32),
            vmem((3 * rows, 128), f32),
            vmem(direction.shape, f32),
            vmem(direction.shape, f32),
            pltpu.SemaphoreType.DMA((9,)),
            pltpu.SemaphoreType.DMA((9,)),
            pltpu.SemaphoreType.DMA((9,)),
        ],
        compiler_params=pltpu.CompilerParams(collective_id=0, has_side_effects=True, vmem_limit_bytes=LIMIT),
        cost_estimate=pl.CostEstimate(flops=200_000, bytes_accessed=400_000, transcendentals=1536),
        name="hessian_apply",
    )(*arguments)
    return pl.pallas_call(
        store,
        out_shape=(
            jax.ShapeDtypeStruct(velocity.shape, f32),
            jax.ShapeDtypeStruct(direction.shape, f32),
        ),
        in_specs=[pl.BlockSpec(memory_space=vmem)] * 2,
        out_specs=(anywhere,) * 2,
        scratch_shapes=[pltpu.SemaphoreType.DMA((2,))],
        compiler_params=pltpu.CompilerParams(vmem_limit_bytes=LIMIT),
        name="store",
    )(image, hess)


def solution(mesh):
    sizes = tuple(mesh.shape[axis] for axis in ("gx", "gy", "gz"))
    return jax.shard_map(
        functools.partial(local, sizes),
        mesh=mesh,
        in_specs=(
            P(None, "gz", "gx", "gy"),
            P(None, "gz", "gx", "gy"),
            P("gz", "gx", "gy"),
            P("gx", "gy"),
            P("gx", "gy"),
            P(),
            P("gx", ("gy", "gz")),
            P("gx", ("gy", "gz")),
            P("gx", ("gy", "gz")),
        ),
        out_specs=(P(None, "gz", "gx", "gy"), P("gx", ("gy", "gz"))),
        check_vma=False,
    )
```

```python
import functools

import jax
import jax.numpy as jnp
from jax import lax
from jax.experimental import pallas as pl
from jax.experimental.pallas import tpu as pltpu
from jax.sharding import PartitionSpec as P

NB = 8
REG = 0.05
LIMIT = 4 * 1024 * 1024
MESH = pl.DeviceIdType.MESH
XU, XD, YL, YR, ZZ, ZV, CP, CC, PS = range(9)


def shift(value, by, axis):
    return pltpu.roll(value, by % value.shape[axis], axis)


def kernel(
    sizes,
    vel_h, adj_h, visc_h, flags_h, index_h, table_h, fric_h, mask_h, dir_h,
    out, hess,
    table, vel, adj, flags, index, fric, mask, direc,
    cons, xs_u, xs_d, xr_u, xr_d, zr, yr_l, yr_r, big, cs_p, cs_c, cr_p, cr_c, ps, pr,
    load_sem, send_sem, recv_sem,
):
    ngx, ngy, ngz = sizes
    gx, gy, gz = (lax.axis_index(axis) for axis in ("gx", "gy", "gz"))
    rows, cols = cons.shape[2], cons.shape[3]
    tiles = [slice(128 * m, 128 * (m + 1)) for m in range(3)]
    half = direc.shape[1]
    low = gz == 0
    has_u, has_d = gx > 0, gx < ngx - 1
    has_l, has_r = gy > 0, gy < ngy - 1
    has_c = jnp.where(low, gy, ngy - 1 - gy) > 0
    cross_gy = jnp.where(low, gy + ngy - 1, gy + 1) % ngy

    loads = [
        pltpu.make_async_copy(src, dst, load_sem.at[i])
        for i, (src, dst) in enumerate(
            (
                (table_h, table), (flags_h, flags), (index_h, index), (vel_h, vel), (visc_h, cons.at[:, 3]),
                (dir_h, direc), (adj_h, adj), (fric_h, fric), (mask_h, mask),
            )
        )
    ]
    for load in loads[:5]:
        load.start()

    up = {"gx": (gx + ngx - 1) % ngx}
    down = {"gx": (gx + 1) % ngx}
    left = {"gy": (gy + ngy - 1) % ngy}
    right = {"gy": (gy + 1) % ngy}
    partner = {"gz": 1 - gz}
    cross = {"gy": cross_gy, "gz": 1 - gz}
    greet = ((has_u, up), (has_d, down), (has_l, left), (has_r, right), (has_c, cross))

    barrier = pltpu.get_barrier_semaphore()
    pl.semaphore_signal(barrier, inc=1, device_id=partner, device_id_type=MESH)
    for has, device in greet:
        @pl.when(has)
        def _():
            pl.semaphore_signal(barrier, inc=1, device_id=device, device_id_type=MESH)

    for load in loads[5:]:
        load.start()

    big[...] = jnp.zeros_like(big)
    for has, buffers in (
        (has_u, (xr_u,)), (has_d, (xr_d,)), (has_l, (yr_l,)), (has_r, (yr_r,)), (has_c, (cr_c,))
    ):
        @pl.when(jnp.logical_not(has))
        def _():
            for buffer in buffers:
                buffer[...] = jnp.zeros_like(buffer)

    def remote(src, dst, at, device):
        return pltpu.make_async_remote_copy(
            src_ref=src, dst_ref=dst, send_sem=send_sem.at[at], recv_sem=recv_sem.at[at],
            device_id=device, device_id_type=MESH,
        )

    to_xu = remote(xs_d, xr_u, XU, down)
    to_xd = remote(xs_u, xr_d, XD, up)
    to_yl = remote(cons.at[:, :, :, cols - 128:], yr_l, YL, right)
    to_yr = remote(cons.at[:, :, :, :128], yr_r, YR, left)
    near, far = 1 - gz, gz
    to_z = remote(vel_h.at[:, near], zr.at[:3], ZZ, partner)
    to_zv = remote(visc_h.at[near], zr.at[3], ZV, partner)
    to_cp = remote(cs_p, cr_p, CP, partner)
    to_cc = remote(cs_c, cr_c, CC, cross)
    to_ps = remote(ps, pr, PS, partner)

    waits = sum((has.astype(jnp.int32) for has, _ in greet), jnp.int32(1))
    pl.semaphore_wait(barrier, waits)
    to_z.start()
    to_zv.start()

    for load in loads[:6]:
        load.wait()
    hanging = flags[...] == 1
    number = index[...]
    chosen = [number == n for n in range(NB)]
    block = [[None] * 3 for _ in range(3)]
    for m in range(3):
        for k in range(3):
            value = jnp.full(number.shape, table[m, k, 0], jnp.float32)
            for n in range(1, NB):
                value = jnp.where(chosen[n], table[m, k, n], value)
            block[m][k] = jnp.where(hanging, value, 1.0 if m == k else 0.0)
    for z in range(2):
        for c in range(3):
            slots = [vel[c, z, :, tile] for tile in tiles]
            for m in range(3):
                cons[z, c, :, tiles[m]] = (
                    block[m][0] * slots[0] + block[m][1] * slots[1] + block[m][2] * slots[2]
                )
    for i, z in enumerate((near, far)):
        for c in range(4):
            at = 4 * i + c
            xs_u[at:at + 1, :cols] = cons[z, c, 0:1, :]
            xs_d[at:at + 1, :cols] = cons[z, c, rows - 1:rows, :]
    for r in range(2):
        for send, row in ((xs_u, r), (xs_d, rows - 2 + r)):
            send[2 * r:2 * r + 1, cols:cols + 128] = direc[row:row + 1, :128]
            send[2 * r + 1:2 * r + 2, cols:cols + half - 128] = direc[row:row + 1, 128:]

    for has, copy in ((has_d, to_xu), (has_u, to_xd), (has_r, to_yl), (has_l, to_yr)):
        @pl.when(has)
        def _():
            copy.start()
    big[rows:2 * rows, 128:128 + half] = direc[...]

    row_at = lax.broadcasted_iota(jnp.int32, (rows, cols), 0)
    lane_at = lax.broadcasted_iota(jnp.int32, (rows, cols), 1)
    inner_row, inner_lane = row_at < rows - 1, lane_at < cols - 1
    own = [[cons[z, c] for c in range(4)] for z in (near, far)]
    total = [[None] * 3 for _ in range(2)]
    visc_z = own[0][3] + own[1][3]
    for c in range(3):
        flux = visc_z * (own[0][c] - own[1][c])
        total[0][c] = flux
        total[1][c] = own[1][3] * own[1][c] - flux
    for i in range(2):
        for axis, inner in ((0, inner_row), (1, inner_lane)):
            visc = own[i][3]
            visc = jnp.where(inner, visc + shift(visc, -1, axis), 0.0)
            for c in range(3):
                a = own[i][c]
                flux = visc * (a - shift(a, -1, axis))
                total[i][c] = total[i][c] + flux - shift(flux, 1, axis)

    for has, copy in ((has_u, to_xu), (has_d, to_xd)):
        @pl.when(has)
        def _():
            copy.wait_recv()
    for buffer, row in ((xr_u, rows - 2), (xr_d, 2 * rows)):
        for r in range(2):
            big[row + r:row + r + 1, 128:256] = buffer[2 * r:2 * r + 1, cols:cols + 128]
            big[row + r:row + r + 1, 256:128 + half] = (
                buffer[2 * r + 1:2 * r + 2, cols:cols + half - 128]
            )
    wide = big[...]
    edge_low, edge_high = wide[:, 128:256], wide[:, half:half + 128]
    cs_p[...] = jnp.where(low, edge_high, edge_low)
    cs_c[...] = jnp.where(low, edge_low, edge_high)
    to_cp.start()

    @pl.when(has_c)
    def _():
        to_cc.start()

    for sent, got, row in ((xs_u, xr_u, 0), (xs_d, xr_d, rows - 1)):
        mine, other = sent[:, :cols], got[:, :cols]
        gap, visc = mine - other, mine + other
        for i in range(2):
            for c in range(3):
                flux = visc[4 * i + 3:4 * i + 4] * gap[4 * i + c:4 * i + c + 1]
                total[i][c] = total[i][c] + jnp.where(row_at == row, flux, 0.0)
    for has, copy in ((has_l, to_yl), (has_r, to_yr)):
        @pl.when(has)
        def _():
            copy.wait_recv()
    total = [[[total[i][c][:, tile] for tile in tiles] for c in range(3)] for i in range(2)]
    lane = lax.broadcasted_iota(jnp.int32, (rows, 128), 1)
    for got, by, at, m in ((yr_l, 1, 0, 0), (yr_r, -1, 127, 2)):
        for i, z in enumerate((near, far)):
            visc = own[i][3][:, tiles[m]] + shift(got[z, 3], by, 1)
            visc = jnp.where(lane == at, visc, 0.0)
            for c in range(3):
                gap = own[i][c][:, tiles[m]] - shift(got[z, c], by, 1)
                total[i][c][m] = total[i][c][m] + visc * gap

    for load in loads[6:]:
        load.wait()
    sums = [None] * 3

    def finish(applied, c, z):
        applied = [0.5 * a for a in applied]
        for k in range(3):
            image = block[0][k] * applied[0] + block[1][k] * applied[1] + block[2][k] * applied[2]
            out[c, z, :, tiles[k]] = image
            term = image * adj[c, z, :, tiles[k]]
            sums[k] = term if sums[k] is None else sums[k] + term

    for c in range(3):
        finish(total[1][c], c, far)
    to_zv.wait_recv()
    visc_z = own[0][3] + zr[3]
    to_z.wait_recv()
    for c in range(3):
        slots = [zr[c, :, tile] for tile in tiles]
        layer = [
            block[m][0] * slots[0] + block[m][1] * slots[1] + block[m][2] * slots[2]
            for m in range(3)
        ]
        finish(
            [
                total[0][c][m] + visc_z[:, tiles[m]] * (own[0][c][:, tiles[m]] - layer[m])
                for m in range(3)
            ],
            c,
            near,
        )
    sums = jnp.concatenate(sums, axis=1)
    first, second = sums[:, :half], sums[:, half:]
    ps[...] = jnp.where(low, second, first)
    to_ps.start()
    mine = jnp.where(low, first, second)

    to_cp.wait_recv()

    @pl.when(has_c)
    def _():
        to_cc.wait_recv()

    from_p, from_c = cr_p[...], cr_c[...]
    from_low = jnp.where(low, from_c, from_p)
    from_high = shift(jnp.where(low, from_p, from_c), half % 128, 1)
    lane = lax.broadcasted_iota(jnp.int32, from_low.shape, 1)
    wide = jnp.concatenate(
        [from_low, wide[:, 128:256], jnp.where(lane < half % 128, wide[:, 256:], from_high)], axis=1
    )

    def laplace(v):
        return 4.0 * v - shift(v, 1, 0) - shift(v, -1, 0) - shift(v, 1, 1) - shift(v, -1, 1)

    row_g = gx * rows - rows + lax.broadcasted_iota(jnp.int32, wide.shape, 0)
    col_g = (gy * ngz + gz) * half - 128 + lax.broadcasted_iota(jnp.int32, wide.shape, 1)
    inside = (row_g >= 0) & (row_g < ngx * rows) & (col_g >= 0) & (col_g < ngy * ngz * half)
    twice = laplace(jnp.where(inside, laplace(wide), 0.0))[rows:2 * rows, 128:128 + half]
    scale = mask[...].astype(jnp.float32) * jnp.exp(fric[...])

    to_ps.wait_recv()
    hess[...] = REG * twice + scale * (mine + pr[...])

    for copy in (to_z, to_zv, to_cp, to_ps):
        copy.wait_send()
    for has, copy in (
        (has_d, to_xu), (has_u, to_xd), (has_r, to_yl), (has_l, to_yr), (has_c, to_cc)
    ):
        @pl.when(has)
        def _():
            copy.wait_send()


def store(image_v, hess_v, image_h, hess_h, sem):
    copies = [
        pltpu.make_async_copy(image_v, image_h, sem.at[0]),
        pltpu.make_async_copy(hess_v, hess_h, sem.at[1]),
    ]
    for copy in copies:
        copy.start()
    for copy in copies:
        copy.wait()


def local(sizes, velocity, adjoint, viscosity, hang_flags, hang_index, block_table, friction, basal_mask, direction):
    _, levels, rows, cols = velocity.shape
    assert levels == 2 and sizes[2] == 2 and cols == 384
    half = direction.shape[1]
    f32 = jnp.float32
    vmem = pltpu.VMEM
    anywhere = pl.BlockSpec(memory_space=pltpu.HBM)
    arguments = [
        pltpu.with_memory_space_constraint(array, pltpu.HBM)
        for array in (
            velocity, adjoint, viscosity, hang_flags, hang_index,
            jnp.transpose(block_table, (1, 2, 0)), friction, basal_mask, direction,
        )
    ]
    image, hess = pl.pallas_call(
        functools.partial(kernel, sizes),
        out_shape=(vmem(velocity.shape, f32), vmem(direction.shape, f32)),
        in_specs=[anywhere] * 9,
        out_specs=(pl.BlockSpec(memory_space=vmem),) * 2,
        scratch_shapes=[
            pltpu.SMEM((3, 3, NB), f32),
            vmem(velocity.shape, f32),
            vmem(velocity.shape, f32),
            vmem(hang_flags.shape, jnp.int32),
            vmem(hang_index.shape, jnp.int32),
            vmem(direction.shape, f32),
            vmem(direction.shape, jnp.int32),
            vmem(direction.shape, f32),
            vmem((levels, 4, rows, cols), f32),
            vmem((8, cols + 128), f32),
            vmem((8, cols + 128), f32),
            vmem((8, cols + 128), f32),
            vmem((8, cols + 128), f32),
            vmem((4, rows, cols), f32),
            vmem((levels, 4, rows, 128), f32),
            vmem((levels, 4, rows, 128), f32),
            vmem((3 * rows, 384), f32),
            vmem((3 * rows, 128), f32),
            vmem((3 * rows, 128), f32),
            vmem((3 * rows, 128), f32),
            vmem((3 * rows, 128), f32),
            vmem(direction.shape, f32),
            vmem(direction.shape, f32),
            pltpu.SemaphoreType.DMA((9,)),
            pltpu.SemaphoreType.DMA((9,)),
            pltpu.SemaphoreType.DMA((9,)),
        ],
        compiler_params=pltpu.CompilerParams(collective_id=0, has_side_effects=True, vmem_limit_bytes=LIMIT),
        cost_estimate=pl.CostEstimate(flops=200_000, bytes_accessed=400_000, transcendentals=1536),
        name="hessian_apply",
    )(*arguments)
    return pl.pallas_call(
        store,
        out_shape=(
            jax.ShapeDtypeStruct(velocity.shape, f32),
            jax.ShapeDtypeStruct(direction.shape, f32),
        ),
        in_specs=[pl.BlockSpec(memory_space=vmem)] * 2,
        out_specs=(anywhere,) * 2,
        scratch_shapes=[pltpu.SemaphoreType.DMA((2,))],
        compiler_params=pltpu.CompilerParams(vmem_limit_bytes=LIMIT),
        name="store",
    )(image, hess)


def solution(mesh):
    sizes = tuple(mesh.shape[axis] for axis in ("gx", "gy", "gz"))
    return jax.shard_map(
        functools.partial(local, sizes),
        mesh=mesh,
        in_specs=(
            P(None, "gz", "gx", "gy"),
            P(None, "gz", "gx", "gy"),
            P("gz", "gx", "gy"),
            P("gx", "gy"),
            P("gx", "gy"),
            P(),
            P("gx", ("gy", "gz")),
            P("gx", ("gy", "gz")),
            P("gx", ("gy", "gz")),
        ),
        out_specs=(P(None, "gz", "gx", "gy"), P("gx", ("gy", "gz"))),
        check_vma=False,
    )
```

```python
import functools

import jax
import jax.numpy as jnp
from jax import lax
from jax.experimental import pallas as pl
from jax.experimental.pallas import tpu as pltpu
from jax.sharding import PartitionSpec as P

NB = 8
REG = 0.05
LIMIT = 4 * 1024 * 1024
MESH = pl.DeviceIdType.MESH
XU, XD, YL, YR, ZZ, CP, CC, PS = range(8)


def shift(value, by, axis):
    return pltpu.roll(value, by % value.shape[axis], axis)


def kernel(
    sizes,
    vel_h, adj_h, visc_h, flags_h, index_h, table_h, fric_h, mask_h, dir_h,
    out, hess,
    table, vel, adj, flags, index, fric, mask, direc,
    cons, xs_u, xs_d, xr_u, xr_d, zr, yr_l, yr_r, big, cs_p, cs_c, cr_p, cr_c, ps, pr,
    load_sem, send_sem, recv_sem,
):
    ngx, ngy, ngz = sizes
    gx, gy, gz = (lax.axis_index(axis) for axis in ("gx", "gy", "gz"))
    rows, cols = cons.shape[2], cons.shape[3]
    tiles = [slice(128 * m, 128 * (m + 1)) for m in range(3)]
    half = direc.shape[1]
    low = gz == 0
    has_u, has_d = gx > 0, gx < ngx - 1
    has_l, has_r = gy > 0, gy < ngy - 1
    has_c = jnp.where(low, gy, ngy - 1 - gy) > 0
    cross_gy = jnp.where(low, gy + ngy - 1, gy + 1) % ngy

    loads = [
        pltpu.make_async_copy(src, dst, load_sem.at[i])
        for i, (src, dst) in enumerate(
            (
                (table_h, table), (flags_h, flags), (index_h, index), (vel_h, vel), (visc_h, cons.at[:, 3]),
                (dir_h, direc), (adj_h, adj), (fric_h, fric), (mask_h, mask),
            )
        )
    ]

    up = {"gx": (gx + ngx - 1) % ngx}
    down = {"gx": (gx + 1) % ngx}
    left = {"gy": (gy + ngy - 1) % ngy}
    right = {"gy": (gy + 1) % ngy}
    partner = {"gz": 1 - gz}
    cross = {"gy": cross_gy, "gz": 1 - gz}
    greet = ((has_u, up), (has_d, down), (has_l, left), (has_r, right), (has_c, cross))

    barrier = pltpu.get_barrier_semaphore()
    pl.semaphore_signal(barrier, inc=1, device_id=partner, device_id_type=MESH)
    for has, device in greet:
        @pl.when(has)
        def _():
            pl.semaphore_signal(barrier, inc=1, device_id=device, device_id_type=MESH)

    for load in loads:
        load.start()

    big[...] = jnp.zeros_like(big)
    for has, buffers in (
        (has_u, (xr_u,)), (has_d, (xr_d,)), (has_l, (yr_l,)), (has_r, (yr_r,)), (has_c, (cr_c,))
    ):
        @pl.when(jnp.logical_not(has))
        def _():
            for buffer in buffers:
                buffer[...] = jnp.zeros_like(buffer)

    def remote(src, dst, at, device):
        return pltpu.make_async_remote_copy(
            src_ref=src, dst_ref=dst, send_sem=send_sem.at[at], recv_sem=recv_sem.at[at],
            device_id=device, device_id_type=MESH,
        )

    to_xu = remote(xs_d, xr_u, XU, down)
    to_xd = remote(xs_u, xr_d, XD, up)
    to_yl = remote(cons.at[:, :, :, cols - 128:], yr_l, YL, right)
    to_yr = remote(cons.at[:, :, :, :128], yr_r, YR, left)
    near, far = 1 - gz, gz
    to_z = remote(cons.at[near], zr, ZZ, partner)
    to_cp = remote(cs_p, cr_p, CP, partner)
    to_cc = remote(cs_c, cr_c, CC, cross)
    to_ps = remote(ps, pr, PS, partner)

    for load in loads[:6]:
        load.wait()
    hanging = flags[...] == 1
    number = index[...]
    chosen = [number == n for n in range(NB)]
    block = [[None] * 3 for _ in range(3)]
    for m in range(3):
        for k in range(3):
            value = jnp.full(number.shape, table[m, k, 0], jnp.float32)
            for n in range(1, NB):
                value = jnp.where(chosen[n], table[m, k, n], value)
            block[m][k] = jnp.where(hanging, value, 1.0 if m == k else 0.0)
    for z in range(2):
        for c in range(3):
            slots = [vel[c, z, :, tile] for tile in tiles]
            for m in range(3):
                cons[z, c, :, tiles[m]] = (
                    block[m][0] * slots[0] + block[m][1] * slots[1] + block[m][2] * slots[2]
                )
    for i, z in enumerate((near, far)):
        for c in range(4):
            at = 4 * i + c
            xs_u[at:at + 1, :cols] = cons[z, c, 0:1, :]
            xs_d[at:at + 1, :cols] = cons[z, c, rows - 1:rows, :]
    for r in range(2):
        for send, row in ((xs_u, r), (xs_d, rows - 2 + r)):
            send[2 * r:2 * r + 1, cols:cols + 128] = direc[row:row + 1, :128]
            send[2 * r + 1:2 * r + 2, cols:cols + half - 128] = direc[row:row + 1, 128:]

    big[rows:2 * rows, 128:128 + half] = direc[...]
    waits = sum((has.astype(jnp.int32) for has, _ in greet), jnp.int32(1))
    pl.semaphore_wait(barrier, waits)
    to_z.start()
    for has, copy in ((has_d, to_xu), (has_u, to_xd), (has_r, to_yl), (has_l, to_yr)):
        @pl.when(has)
        def _():
            copy.start()

    row_at = lax.broadcasted_iota(jnp.int32, (rows, cols), 0)
    lane_at = lax.broadcasted_iota(jnp.int32, (rows, cols), 1)
    inner_row, inner_lane = row_at < rows - 1, lane_at < cols - 1
    own = [[cons[z, c] for c in range(4)] for z in (near, far)]
    total = [[None] * 3 for _ in range(2)]
    visc_z = own[0][3] + own[1][3]
    for c in range(3):
        flux = visc_z * (own[0][c] - own[1][c])
        total[0][c] = flux
        total[1][c] = own[1][3] * own[1][c] - flux
    for i in range(2):
        for axis, inner in ((0, inner_row), (1, inner_lane)):
            visc = own[i][3]
            visc = jnp.where(inner, visc + shift(visc, -1, axis), 0.0)
            for c in range(3):
                a = own[i][c]
                flux = visc * (a - shift(a, -1, axis))
                total[i][c] = total[i][c] + flux - shift(flux, 1, axis)

    for has, copy in ((has_u, to_xu), (has_d, to_xd)):
        @pl.when(has)
        def _():
            copy.wait_recv()
    for buffer, row in ((xr_u, rows - 2), (xr_d, 2 * rows)):
        for r in range(2):
            big[row + r:row + r + 1, 128:256] = buffer[2 * r:2 * r + 1, cols:cols + 128]
            big[row + r:row + r + 1, 256:128 + half] = (
                buffer[2 * r + 1:2 * r + 2, cols:cols + half - 128]
            )
    wide = big[...]
    edge_low, edge_high = wide[:, 128:256], wide[:, half:half + 128]
    cs_p[...] = jnp.where(low, edge_high, edge_low)
    cs_c[...] = jnp.where(low, edge_low, edge_high)
    to_cp.start()

    @pl.when(has_c)
    def _():
        to_cc.start()

    for sent, got, row in ((xs_u, xr_u, 0), (xs_d, xr_d, rows - 1)):
        mine, other = sent[:, :cols], got[:, :cols]
        gap, visc = mine - other, mine + other
        for i in range(2):
            for c in range(3):
                flux = visc[4 * i + 3:4 * i + 4] * gap[4 * i + c:4 * i + c + 1]
                total[i][c] = total[i][c] + jnp.where(row_at == row, flux, 0.0)
    for has, copy in ((has_l, to_yl), (has_r, to_yr)):
        @pl.when(has)
        def _():
            copy.wait_recv()
    total = [[[total[i][c][:, tile] for tile in tiles] for c in range(3)] for i in range(2)]
    lane = lax.broadcasted_iota(jnp.int32, (rows, 128), 1)
    for got, by, at, m in ((yr_l, 1, 0, 0), (yr_r, -1, 127, 2)):
        for i, z in enumerate((near, far)):
            visc = own[i][3][:, tiles[m]] + shift(got[z, 3], by, 1)
            visc = jnp.where(lane == at, visc, 0.0)
            for c in range(3):
                gap = own[i][c][:, tiles[m]] - shift(got[z, c], by, 1)
                total[i][c][m] = total[i][c][m] + visc * gap

    for load in loads[6:]:
        load.wait()
    sums = [None] * 3

    def finish(applied, c, z):
        applied = [0.5 * a for a in applied]
        for k in range(3):
            image = block[0][k] * applied[0] + block[1][k] * applied[1] + block[2][k] * applied[2]
            out[c, z, :, tiles[k]] = image
            term = image * adj[c, z, :, tiles[k]]
            sums[k] = term if sums[k] is None else sums[k] + term

    for c in range(3):
        finish(total[1][c], c, far)
    to_z.wait_recv()
    visc_z = own[0][3] + zr[3]
    for c in range(3):
        flux = visc_z * (own[0][c] - zr[c])
        finish([total[0][c][m] + flux[:, tiles[m]] for m in range(3)], c, near)
    sums = jnp.concatenate(sums, axis=1)
    first, second = sums[:, :half], sums[:, half:]
    ps[...] = jnp.where(low, second, first)
    to_ps.start()
    mine = jnp.where(low, first, second)

    to_cp.wait_recv()

    @pl.when(has_c)
    def _():
        to_cc.wait_recv()

    from_p, from_c = cr_p[...], cr_c[...]
    from_low = jnp.where(low, from_c, from_p)
    from_high = shift(jnp.where(low, from_p, from_c), half % 128, 1)
    lane = lax.broadcasted_iota(jnp.int32, from_low.shape, 1)
    wide = jnp.concatenate(
        [from_low, wide[:, 128:256], jnp.where(lane < half % 128, wide[:, 256:], from_high)], axis=1
    )

    def laplace(v):
        return 4.0 * v - shift(v, 1, 0) - shift(v, -1, 0) - shift(v, 1, 1) - shift(v, -1, 1)

    row_g = gx * rows - rows + lax.broadcasted_iota(jnp.int32, wide.shape, 0)
    col_g = (gy * ngz + gz) * half - 128 + lax.broadcasted_iota(jnp.int32, wide.shape, 1)
    inside = (row_g >= 0) & (row_g < ngx * rows) & (col_g >= 0) & (col_g < ngy * ngz * half)
    twice = laplace(jnp.where(inside, laplace(wide), 0.0))[rows:2 * rows, 128:128 + half]
    scale = mask[...].astype(jnp.float32) * jnp.exp(fric[...])

    to_ps.wait_recv()
    hess[...] = REG * twice + scale * (mine + pr[...])

    for copy in (to_z, to_cp, to_ps):
        copy.wait_send()
    for has, copy in (
        (has_d, to_xu), (has_u, to_xd), (has_r, to_yl), (has_l, to_yr), (has_c, to_cc)
    ):
        @pl.when(has)
        def _():
            copy.wait_send()


def store(image_v, hess_v, image_h, hess_h, sem):
    copies = [
        pltpu.make_async_copy(image_v, image_h, sem.at[0]),
        pltpu.make_async_copy(hess_v, hess_h, sem.at[1]),
    ]
    for copy in copies:
        copy.start()
    for copy in copies:
        copy.wait()


def local(sizes, velocity, adjoint, viscosity, hang_flags, hang_index, block_table, friction, basal_mask, direction):
    _, levels, rows, cols = velocity.shape
    assert levels == 2 and sizes[2] == 2 and cols == 384
    half = direction.shape[1]
    f32 = jnp.float32
    vmem = pltpu.VMEM
    anywhere = pl.BlockSpec(memory_space=pltpu.HBM)
    arguments = [
        pltpu.with_memory_space_constraint(array, pltpu.HBM)
        for array in (
            velocity, adjoint, viscosity, hang_flags, hang_index,
            jnp.transpose(block_table, (1, 2, 0)), friction, basal_mask, direction,
        )
    ]
    image, hess = pl.pallas_call(
        functools.partial(kernel, sizes),
        out_shape=(vmem(velocity.shape, f32), vmem(direction.shape, f32)),
        in_specs=[anywhere] * 9,
        out_specs=(pl.BlockSpec(memory_space=vmem),) * 2,
        scratch_shapes=[
            pltpu.SMEM((3, 3, NB), f32),
            vmem(velocity.shape, f32),
            vmem(velocity.shape, f32),
            vmem(hang_flags.shape, jnp.int32),
            vmem(hang_index.shape, jnp.int32),
            vmem(direction.shape, f32),
            vmem(direction.shape, jnp.int32),
            vmem(direction.shape, f32),
            vmem((levels, 4, rows, cols), f32),
            vmem((8, cols + 128), f32),
            vmem((8, cols + 128), f32),
            vmem((8, cols + 128), f32),
            vmem((8, cols + 128), f32),
            vmem((4, rows, cols), f32),
            vmem((levels, 4, rows, 128), f32),
            vmem((levels, 4, rows, 128), f32),
            vmem((3 * rows, 384), f32),
            vmem((3 * rows, 128), f32),
            vmem((3 * rows, 128), f32),
            vmem((3 * rows, 128), f32),
            vmem((3 * rows, 128), f32),
            vmem(direction.shape, f32),
            vmem(direction.shape, f32),
            pltpu.SemaphoreType.DMA((9,)),
            pltpu.SemaphoreType.DMA((8,)),
            pltpu.SemaphoreType.DMA((8,)),
        ],
        compiler_params=pltpu.CompilerParams(collective_id=0, has_side_effects=True, vmem_limit_bytes=LIMIT),
        cost_estimate=pl.CostEstimate(flops=200_000, bytes_accessed=400_000, transcendentals=1536),
        name="hessian_apply",
    )(*arguments)
    return pl.pallas_call(
        store,
        out_shape=(
            jax.ShapeDtypeStruct(velocity.shape, f32),
            jax.ShapeDtypeStruct(direction.shape, f32),
        ),
        in_specs=[pl.BlockSpec(memory_space=vmem)] * 2,
        out_specs=(anywhere,) * 2,
        scratch_shapes=[pltpu.SemaphoreType.DMA((2,))],
        compiler_params=pltpu.CompilerParams(vmem_limit_bytes=LIMIT),
        name="store",
    )(image, hess)


def solution(mesh):
    sizes = tuple(mesh.shape[axis] for axis in ("gx", "gy", "gz"))
    return jax.shard_map(
        functools.partial(local, sizes),
        mesh=mesh,
        in_specs=(
            P(None, "gz", "gx", "gy"),
            P(None, "gz", "gx", "gy"),
            P("gz", "gx", "gy"),
            P("gx", "gy"),
            P("gx", "gy"),
            P(),
            P("gx", ("gy", "gz")),
            P("gx", ("gy", "gz")),
            P("gx", ("gy", "gz")),
        ),
        out_specs=(P(None, "gz", "gx", "gy"), P("gx", ("gy", "gz"))),
        check_vma=False,
    )
```

```python
import functools

import jax
import jax.numpy as jnp
from jax import lax
from jax.experimental import pallas as pl
from jax.experimental.pallas import tpu as pltpu
from jax.sharding import PartitionSpec as P

NB = 8
REG = 0.05
LIMIT = 4 * 1024 * 1024
MESH = pl.DeviceIdType.MESH
XU, XD, YL, YR, ZZ, CP, CC, PS = range(8)


def shift(value, by, axis):
    return pltpu.roll(value, by % value.shape[axis], axis)


def kernel(
    sizes,
    vel_h, adj_h, visc_h, flags_h, index_h, table_h, fric_h, mask_h, dir_h,
    out, hess,
    table, vel, adj, flags, index, fric, mask, direc,
    cons, xs_u, xs_d, xr_u, xr_d, zr, yr_l, yr_r, big, cs_p, cs_c, cr_p, cr_c, ps, pr,
    load_sem, send_sem, recv_sem,
):
    ngx, ngy, ngz = sizes
    gx, gy, gz = (lax.axis_index(axis) for axis in ("gx", "gy", "gz"))
    rows, cols = cons.shape[2], cons.shape[3]
    tiles = [slice(128 * m, 128 * (m + 1)) for m in range(3)]
    half = direc.shape[1]
    low = gz == 0
    has_u, has_d = gx > 0, gx < ngx - 1
    has_l, has_r = gy > 0, gy < ngy - 1
    has_c = jnp.where(low, gy, ngy - 1 - gy) > 0
    cross_gy = jnp.where(low, gy + ngy - 1, gy + 1) % ngy

    loads = [
        pltpu.make_async_copy(src, dst, load_sem.at[i])
        for i, (src, dst) in enumerate(
            (
                (table_h, table), (flags_h, flags), (index_h, index), (vel_h, vel), (visc_h, cons.at[:, 3]),
                (dir_h, direc), (adj_h, adj), (fric_h, fric), (mask_h, mask),
            )
        )
    ]

    up = {"gx": (gx + ngx - 1) % ngx}
    down = {"gx": (gx + 1) % ngx}
    left = {"gy": (gy + ngy - 1) % ngy}
    right = {"gy": (gy + 1) % ngy}
    partner = {"gz": 1 - gz}
    cross = {"gy": cross_gy, "gz": 1 - gz}
    greet = ((has_u, up), (has_d, down), (has_l, left), (has_r, right), (has_c, cross))

    barrier = pltpu.get_barrier_semaphore()
    pl.semaphore_signal(barrier, inc=1, device_id=partner, device_id_type=MESH)
    for has, device in greet:
        @pl.when(has)
        def _():
            pl.semaphore_signal(barrier, inc=1, device_id=device, device_id_type=MESH)

    for load in loads:
        load.start()

    big[...] = jnp.zeros_like(big)
    for has, buffers in (
        (has_u, (xr_u,)), (has_d, (xr_d,)), (has_l, (yr_l,)), (has_r, (yr_r,)), (has_c, (cr_c,))
    ):
        @pl.when(jnp.logical_not(has))
        def _():
            for buffer in buffers:
                buffer[...] = jnp.zeros_like(buffer)

    def remote(src, dst, at, device):
        return pltpu.make_async_remote_copy(
            src_ref=src, dst_ref=dst, send_sem=send_sem.at[at], recv_sem=recv_sem.at[at],
            device_id=device, device_id_type=MESH,
        )

    to_xu = remote(xs_d, xr_u, XU, down)
    to_xd = remote(xs_u, xr_d, XD, up)
    to_yl = remote(cons.at[:, :, :, cols - 128:], yr_l, YL, right)
    to_yr = remote(cons.at[:, :, :, :128], yr_r, YR, left)
    near, far = 1 - gz, gz
    to_z = remote(cons.at[near], zr, ZZ, partner)
    to_cp = remote(cs_p, cr_p, CP, partner)
    to_cc = remote(cs_c, cr_c, CC, cross)
    to_ps = remote(ps, pr, PS, partner)

    for load in loads[:6]:
        load.wait()
    hanging = flags[...] == 1
    number = index[...]
    chosen = [number == n for n in range(NB)]
    block = [[None] * 3 for _ in range(3)]
    for m in range(3):
        for k in range(3):
            value = jnp.full(number.shape, table[m, k, 0], jnp.float32)
            for n in range(1, NB):
                value = jnp.where(chosen[n], table[m, k, n], value)
            block[m][k] = jnp.where(hanging, value, 1.0 if m == k else 0.0)
    for z in range(2):
        for c in range(3):
            slots = [vel[c, z, :, tile] for tile in tiles]
            for m in range(3):
                cons[z, c, :, tiles[m]] = (
                    block[m][0] * slots[0] + block[m][1] * slots[1] + block[m][2] * slots[2]
                )
    for i, z in enumerate((near, far)):
        for c in range(4):
            at = 4 * i + c
            xs_u[at:at + 1, :cols] = cons[z, c, 0:1, :]
            xs_d[at:at + 1, :cols] = cons[z, c, rows - 1:rows, :]
    for r in range(2):
        for send, row in ((xs_u, r), (xs_d, rows - 2 + r)):
            send[2 * r:2 * r + 1, cols:cols + 128] = direc[row:row + 1, :128]
            send[2 * r + 1:2 * r + 2, cols:cols + half - 128] = direc[row:row + 1, 128:]

    big[rows:2 * rows, 128:128 + half] = direc[...]
    waits = sum((has.astype(jnp.int32) for has, _ in greet), jnp.int32(1))
    pl.semaphore_wait(barrier, waits)
    to_z.start()
    for has, copy in ((has_d, to_xu), (has_u, to_xd), (has_r, to_yl), (has_l, to_yr)):
        @pl.when(has)
        def _():
            copy.start()

    row_at = lax.broadcasted_iota(jnp.int32, (rows, cols), 0)
    lane_at = lax.broadcasted_iota(jnp.int32, (rows, cols), 1)
    inner_row, inner_lane = row_at < rows - 1, lane_at < cols - 1
    own = [[cons[z, c] for c in range(4)] for z in (near, far)]
    total = [[None] * 3 for _ in range(2)]
    visc_z = own[0][3] + own[1][3]
    for c in range(3):
        flux = visc_z * (own[0][c] - own[1][c])
        total[0][c] = flux
        total[1][c] = own[1][3] * own[1][c] - flux
    for i in range(2):
        for axis, inner in ((0, inner_row), (1, inner_lane)):
            visc = own[i][3]
            visc = jnp.where(inner, visc + shift(visc, -1, axis), 0.0)
            for c in range(3):
                a = own[i][c]
                flux = visc * (a - shift(a, -1, axis))
                total[i][c] = total[i][c] + flux - shift(flux, 1, axis)

    for has, copy in ((has_u, to_xu), (has_d, to_xd)):
        @pl.when(has)
        def _():
            copy.wait_recv()
    for buffer, row in ((xr_u, rows - 2), (xr_d, 2 * rows)):
        for r in range(2):
            big[row + r:row + r + 1, 128:256] = buffer[2 * r:2 * r + 1, cols:cols + 128]
            big[row + r:row + r + 1, 256:128 + half] = (
                buffer[2 * r + 1:2 * r + 2, cols:cols + half - 128]
            )
    wide = big[...]
    edge_low, edge_high = wide[:, 128:256], wide[:, half:half + 128]
    cs_p[...] = jnp.where(low, edge_high, edge_low)
    cs_c[...] = jnp.where(low, edge_low, edge_high)
    to_cp.start()

    @pl.when(has_c)
    def _():
        to_cc.start()

    for sent, got, row in ((xs_u, xr_u, 0), (xs_d, xr_d, rows - 1)):
        mine, other = sent[:, :cols], got[:, :cols]
        gap, visc = mine - other, mine + other
        for i in range(2):
            for c in range(3):
                flux = visc[4 * i + 3:4 * i + 4] * gap[4 * i + c:4 * i + c + 1]
                total[i][c] = total[i][c] + jnp.where(row_at == row, flux, 0.0)
    for has, copy in ((has_l, to_yl), (has_r, to_yr)):
        @pl.when(has)
        def _():
            copy.wait_recv()
    total = [[[total[i][c][:, tile] for tile in tiles] for c in range(3)] for i in range(2)]
    lane = lax.broadcasted_iota(jnp.int32, (rows, 128), 1)
    for got, by, at, m in ((yr_l, 1, 0, 0), (yr_r, -1, 127, 2)):
        for i, z in enumerate((near, far)):
            visc = own[i][3][:, tiles[m]] + shift(got[z, 3], by, 1)
            visc = jnp.where(lane == at, visc, 0.0)
            for c in range(3):
                gap = own[i][c][:, tiles[m]] - shift(got[z, c], by, 1)
                total[i][c][m] = total[i][c][m] + visc * gap

    for load in loads[6:]:
        load.wait()
    sums = [None] * 3

    def finish(applied, c, z):
        applied = [0.5 * a for a in applied]
        for k in range(3):
            image = block[0][k] * applied[0] + block[1][k] * applied[1] + block[2][k] * applied[2]
            out[c, z, :, tiles[k]] = image
            term = image * adj[c, z, :, tiles[k]]
            sums[k] = term if sums[k] is None else sums[k] + term

    for c in range(3):
        finish(total[1][c], c, far)
    to_z.wait_recv()
    visc_z = own[0][3] + zr[3]
    for c in range(3):
        flux = visc_z * (own[0][c] - zr[c])
        finish([total[0][c][m] + flux[:, tiles[m]] for m in range(3)], c, near)
    sums = jnp.concatenate(sums, axis=1)
    first, second = sums[:, :half], sums[:, half:]
    ps[...] = jnp.where(low, second, first)
    to_ps.start()
    mine = jnp.where(low, first, second)

    scale = mask[...].astype(jnp.float32) * jnp.exp(fric[...])
    row_g = gx * rows - rows + lax.broadcasted_iota(jnp.int32, wide.shape, 0)
    col_g = (gy * ngz + gz) * half - 128 + lax.broadcasted_iota(jnp.int32, wide.shape, 1)
    inside = (row_g >= 0) & (row_g < ngx * rows) & (col_g >= 0) & (col_g < ngy * ngz * half)
    base = scale * mine
    to_z.wait_send()
    for has, copy in ((has_d, to_xu), (has_u, to_xd), (has_r, to_yl), (has_l, to_yr)):
        @pl.when(has)
        def _():
            copy.wait_send()
    to_cp.wait_recv()

    @pl.when(has_c)
    def _():
        to_cc.wait_recv()

    from_p, from_c = cr_p[...], cr_c[...]
    from_low = jnp.where(low, from_c, from_p)
    from_high = shift(jnp.where(low, from_p, from_c), half % 128, 1)
    lane = lax.broadcasted_iota(jnp.int32, from_low.shape, 1)
    wide = jnp.concatenate(
        [from_low, wide[:, 128:256], jnp.where(lane < half % 128, wide[:, 256:], from_high)], axis=1
    )

    def laplace(v):
        return 4.0 * v - shift(v, 1, 0) - shift(v, -1, 0) - shift(v, 1, 1) - shift(v, -1, 1)

    twice = laplace(jnp.where(inside, laplace(wide), 0.0))[rows:2 * rows, 128:128 + half]

    base = REG * twice + base
    to_cp.wait_send()

    @pl.when(has_c)
    def _():
        to_cc.wait_send()

    to_ps.wait_send()
    to_ps.wait_recv()
    hess[...] = base + scale * pr[...]


def store(image_v, hess_v, image_h, hess_h, sem):
    copies = [
        pltpu.make_async_copy(image_v, image_h, sem.at[0]),
        pltpu.make_async_copy(hess_v, hess_h, sem.at[1]),
    ]
    for copy in copies:
        copy.start()
    for copy in copies:
        copy.wait()


def local(sizes, velocity, adjoint, viscosity, hang_flags, hang_index, block_table, friction, basal_mask, direction):
    _, levels, rows, cols = velocity.shape
    assert levels == 2 and sizes[2] == 2 and cols == 384
    half = direction.shape[1]
    f32 = jnp.float32
    vmem = pltpu.VMEM
    anywhere = pl.BlockSpec(memory_space=pltpu.HBM)
    arguments = [
        pltpu.with_memory_space_constraint(array, pltpu.HBM)
        for array in (
            velocity, adjoint, viscosity, hang_flags, hang_index,
            jnp.transpose(block_table, (1, 2, 0)), friction, basal_mask, direction,
        )
    ]
    image, hess = pl.pallas_call(
        functools.partial(kernel, sizes),
        out_shape=(vmem(velocity.shape, f32), vmem(direction.shape, f32)),
        in_specs=[anywhere] * 9,
        out_specs=(pl.BlockSpec(memory_space=vmem),) * 2,
        scratch_shapes=[
            pltpu.SMEM((3, 3, NB), f32),
            vmem(velocity.shape, f32),
            vmem(velocity.shape, f32),
            vmem(hang_flags.shape, jnp.int32),
            vmem(hang_index.shape, jnp.int32),
            vmem(direction.shape, f32),
            vmem(direction.shape, jnp.int32),
            vmem(direction.shape, f32),
            vmem((levels, 4, rows, cols), f32),
            vmem((8, cols + 128), f32),
            vmem((8, cols + 128), f32),
            vmem((8, cols + 128), f32),
            vmem((8, cols + 128), f32),
            vmem((4, rows, cols), f32),
            vmem((levels, 4, rows, 128), f32),
            vmem((levels, 4, rows, 128), f32),
            vmem((3 * rows, 384), f32),
            vmem((3 * rows, 128), f32),
            vmem((3 * rows, 128), f32),
            vmem((3 * rows, 128), f32),
            vmem((3 * rows, 128), f32),
            vmem(direction.shape, f32),
            vmem(direction.shape, f32),
            pltpu.SemaphoreType.DMA((9,)),
            pltpu.SemaphoreType.DMA((8,)),
            pltpu.SemaphoreType.DMA((8,)),
        ],
        compiler_params=pltpu.CompilerParams(collective_id=0, has_side_effects=True, vmem_limit_bytes=LIMIT),
        cost_estimate=pl.CostEstimate(flops=200_000, bytes_accessed=400_000, transcendentals=1536),
        name="hessian_apply",
    )(*arguments)
    return pl.pallas_call(
        store,
        out_shape=(
            jax.ShapeDtypeStruct(velocity.shape, f32),
            jax.ShapeDtypeStruct(direction.shape, f32),
        ),
        in_specs=[pl.BlockSpec(memory_space=vmem)] * 2,
        out_specs=(anywhere,) * 2,
        scratch_shapes=[pltpu.SemaphoreType.DMA((2,))],
        compiler_params=pltpu.CompilerParams(vmem_limit_bytes=LIMIT),
        name="store",
    )(image, hess)


def solution(mesh):
    sizes = tuple(mesh.shape[axis] for axis in ("gx", "gy", "gz"))
    return jax.shard_map(
        functools.partial(local, sizes),
        mesh=mesh,
        in_specs=(
            P(None, "gz", "gx", "gy"),
            P(None, "gz", "gx", "gy"),
            P("gz", "gx", "gy"),
            P("gx", "gy"),
            P("gx", "gy"),
            P(),
            P("gx", ("gy", "gz")),
            P("gx", ("gy", "gz")),
            P("gx", ("gy", "gz")),
        ),
        out_specs=(P(None, "gz", "gx", "gy"), P("gx", ("gy", "gz"))),
        check_vma=False,
    )
```

```python
import functools

import jax
import jax.numpy as jnp
from jax import lax
from jax.experimental import pallas as pl
from jax.experimental.pallas import tpu as pltpu
from jax.sharding import PartitionSpec as P

NB = 8
REG = 0.05
LIMIT = 4 * 1024 * 1024
MESH = pl.DeviceIdType.MESH
XU, XD, YL, YR, CP, CC, PS, ZZ = range(8)


def shift(value, by, axis):
    return pltpu.roll(value, by % value.shape[axis], axis)


def kernel(
    sizes,
    vel_h, adj_h, visc_h, flags_h, index_h, table_h, fric_h, mask_h, dir_h,
    out, hess,
    table, vel, adj, flags, index, fric, mask, direc,
    cons, xs_u, xs_d, xr_u, xr_d, zr, yr_l, yr_r, big, cs_p, cs_c, cr_p, cr_c, ps, pr,
    load_sem, send_sem, recv_sem,
):
    ngx, ngy, ngz = sizes
    gx, gy, gz = (lax.axis_index(axis) for axis in ("gx", "gy", "gz"))
    rows, cols = cons.shape[2], cons.shape[3]
    tiles = [slice(128 * m, 128 * (m + 1)) for m in range(3)]
    half = direc.shape[1]
    low = gz == 0
    has_u, has_d = gx > 0, gx < ngx - 1
    has_l, has_r = gy > 0, gy < ngy - 1
    has_c = jnp.where(low, gy, ngy - 1 - gy) > 0
    cross_gy = jnp.where(low, gy + ngy - 1, gy + 1) % ngy

    loads = [
        pltpu.make_async_copy(src, dst, load_sem.at[i])
        for i, (src, dst) in enumerate(
            (
                (table_h, table), (flags_h, flags), (index_h, index), (vel_h, vel), (visc_h, cons.at[:, 3]),
                (dir_h, direc), (adj_h, adj), (fric_h, fric), (mask_h, mask),
            )
        )
    ]

    up = {"gx": (gx + ngx - 1) % ngx}
    down = {"gx": (gx + 1) % ngx}
    left = {"gy": (gy + ngy - 1) % ngy}
    right = {"gy": (gy + 1) % ngy}
    partner = {"gz": 1 - gz}
    cross = {"gy": cross_gy, "gz": 1 - gz}
    greet = ((has_u, up), (has_d, down), (has_l, left), (has_r, right), (has_c, cross))

    barrier = pltpu.get_barrier_semaphore()
    pl.semaphore_signal(barrier, inc=1, device_id=partner, device_id_type=MESH)
    for has, device in greet:
        @pl.when(has)
        def _():
            pl.semaphore_signal(barrier, inc=1, device_id=device, device_id_type=MESH)

    for load in loads:
        load.start()

    big[...] = jnp.zeros_like(big)
    for has, buffers in (
        (has_u, (xr_u,)), (has_d, (xr_d,)), (has_l, (yr_l,)), (has_r, (yr_r,)), (has_c, (cr_c,))
    ):
        @pl.when(jnp.logical_not(has))
        def _():
            for buffer in buffers:
                buffer[...] = jnp.zeros_like(buffer)

    def remote(src, dst, at, device):
        return pltpu.make_async_remote_copy(
            src_ref=src, dst_ref=dst, send_sem=send_sem.at[at], recv_sem=recv_sem.at[at],
            device_id=device, device_id_type=MESH,
        )

    to_xu = remote(xs_d, xr_u, XU, down)
    to_xd = remote(xs_u, xr_d, XD, up)
    to_yl = remote(cons.at[:, :, :, cols - 128:], yr_l, YL, right)
    to_yr = remote(cons.at[:, :, :, :128], yr_r, YR, left)
    near, far = 1 - gz, gz
    to_z = [remote(cons.at[near, c], zr.at[c], ZZ + c, partner) for c in range(4)]
    to_cp = remote(cs_p, cr_p, CP, partner)
    to_cc = remote(cs_c, cr_c, CC, cross)
    to_ps = remote(ps, pr, PS, partner)

    for load in loads[:6]:
        load.wait()
    hanging = flags[...] == 1
    number = index[...]
    chosen = [number == n for n in range(NB)]
    block = [[None] * 3 for _ in range(3)]
    for m in range(3):
        for k in range(3):
            value = jnp.full(number.shape, table[m, k, 0], jnp.float32)
            for n in range(1, NB):
                value = jnp.where(chosen[n], table[m, k, n], value)
            block[m][k] = jnp.where(hanging, value, 1.0 if m == k else 0.0)
    for z in range(2):
        for c in range(3):
            slots = [vel[c, z, :, tile] for tile in tiles]
            for m in range(3):
                cons[z, c, :, tiles[m]] = (
                    block[m][0] * slots[0] + block[m][1] * slots[1] + block[m][2] * slots[2]
                )
    for i, z in enumerate((near, far)):
        for c in range(4):
            at = 4 * i + c
            xs_u[at:at + 1, :cols] = cons[z, c, 0:1, :]
            xs_d[at:at + 1, :cols] = cons[z, c, rows - 1:rows, :]
    for r in range(2):
        for send, row in ((xs_u, r), (xs_d, rows - 2 + r)):
            send[2 * r:2 * r + 1, cols:cols + 128] = direc[row:row + 1, :128]
            send[2 * r + 1:2 * r + 2, cols:cols + half - 128] = direc[row:row + 1, 128:]

    big[rows:2 * rows, 128:128 + half] = direc[...]
    waits = sum((has.astype(jnp.int32) for has, _ in greet), jnp.int32(1))
    pl.semaphore_wait(barrier, waits)
    for c in (3, 0, 1, 2):
        to_z[c].start()
    for has, copy in ((has_d, to_xu), (has_u, to_xd), (has_r, to_yl), (has_l, to_yr)):
        @pl.when(has)
        def _():
            copy.start()

    row_at = lax.broadcasted_iota(jnp.int32, (rows, cols), 0)
    lane_at = lax.broadcasted_iota(jnp.int32, (rows, cols), 1)
    inner_row, inner_lane = row_at < rows - 1, lane_at < cols - 1
    own = [[cons[z, c] for c in range(4)] for z in (near, far)]
    total = [[None] * 3 for _ in range(2)]
    visc_z = own[0][3] + own[1][3]
    for c in range(3):
        flux = visc_z * (own[0][c] - own[1][c])
        total[0][c] = flux
        total[1][c] = own[1][3] * own[1][c] - flux
    for i in range(2):
        for axis, inner in ((0, inner_row), (1, inner_lane)):
            visc = own[i][3]
            visc = jnp.where(inner, visc + shift(visc, -1, axis), 0.0)
            for c in range(3):
                a = own[i][c]
                flux = visc * (a - shift(a, -1, axis))
                total[i][c] = total[i][c] + flux - shift(flux, 1, axis)

    for has, copy in ((has_u, to_xu), (has_d, to_xd)):
        @pl.when(has)
        def _():
            copy.wait_recv()
    for buffer, row in ((xr_u, rows - 2), (xr_d, 2 * rows)):
        for r in range(2):
            big[row + r:row + r + 1, 128:256] = buffer[2 * r:2 * r + 1, cols:cols + 128]
            big[row + r:row + r + 1, 256:128 + half] = (
                buffer[2 * r + 1:2 * r + 2, cols:cols + half - 128]
            )
    wide = big[...]
    edge_low, edge_high = wide[:, 128:256], wide[:, half:half + 128]
    cs_p[...] = jnp.where(low, edge_high, edge_low)
    cs_c[...] = jnp.where(low, edge_low, edge_high)
    to_cp.start()

    @pl.when(has_c)
    def _():
        to_cc.start()

    for sent, got, row in ((xs_u, xr_u, 0), (xs_d, xr_d, rows - 1)):
        mine, other = sent[:, :cols], got[:, :cols]
        gap, visc = mine - other, mine + other
        for i in range(2):
            for c in range(3):
                flux = visc[4 * i + 3:4 * i + 4] * gap[4 * i + c:4 * i + c + 1]
                total[i][c] = total[i][c] + jnp.where(row_at == row, flux, 0.0)
    for has, copy in ((has_l, to_yl), (has_r, to_yr)):
        @pl.when(has)
        def _():
            copy.wait_recv()
    total = [[[total[i][c][:, tile] for tile in tiles] for c in range(3)] for i in range(2)]
    lane = lax.broadcasted_iota(jnp.int32, (rows, 128), 1)
    for got, by, at, m in ((yr_l, 1, 0, 0), (yr_r, -1, 127, 2)):
        for i, z in enumerate((near, far)):
            visc = own[i][3][:, tiles[m]] + shift(got[z, 3], by, 1)
            visc = jnp.where(lane == at, visc, 0.0)
            for c in range(3):
                gap = own[i][c][:, tiles[m]] - shift(got[z, c], by, 1)
                total[i][c][m] = total[i][c][m] + visc * gap

    for load in loads[6:]:
        load.wait()
    sums = [None] * 3

    def finish(applied, c, z):
        applied = [0.5 * a for a in applied]
        for k in range(3):
            image = block[0][k] * applied[0] + block[1][k] * applied[1] + block[2][k] * applied[2]
            out[c, z, :, tiles[k]] = image
            term = image * adj[c, z, :, tiles[k]]
            sums[k] = term if sums[k] is None else sums[k] + term

    for c in range(3):
        finish(total[1][c], c, far)
    to_z[3].wait_recv()
    visc_z = own[0][3] + zr[3]
    for c in range(3):
        to_z[c].wait_recv()
        flux = visc_z * (own[0][c] - zr[c])
        finish([total[0][c][m] + flux[:, tiles[m]] for m in range(3)], c, near)
    sums = jnp.concatenate(sums, axis=1)
    first, second = sums[:, :half], sums[:, half:]
    ps[...] = jnp.where(low, second, first)
    to_ps.start()
    mine = jnp.where(low, first, second)

    scale = mask[...].astype(jnp.float32) * jnp.exp(fric[...])
    row_g = gx * rows - rows + lax.broadcasted_iota(jnp.int32, wide.shape, 0)
    col_g = (gy * ngz + gz) * half - 128 + lax.broadcasted_iota(jnp.int32, wide.shape, 1)
    inside = (row_g >= 0) & (row_g < ngx * rows) & (col_g >= 0) & (col_g < ngy * ngz * half)
    base = scale * mine
    for copy in to_z:
        copy.wait_send()
    for has, copy in ((has_d, to_xu), (has_u, to_xd), (has_r, to_yl), (has_l, to_yr)):
        @pl.when(has)
        def _():
            copy.wait_send()
    to_cp.wait_recv()

    @pl.when(has_c)
    def _():
        to_cc.wait_recv()

    from_p, from_c = cr_p[...], cr_c[...]
    from_low = jnp.where(low, from_c, from_p)
    from_high = shift(jnp.where(low, from_p, from_c), half % 128, 1)
    lane = lax.broadcasted_iota(jnp.int32, from_low.shape, 1)
    wide = jnp.concatenate(
        [from_low, wide[:, 128:256], jnp.where(lane < half % 128, wide[:, 256:], from_high)], axis=1
    )

    def laplace(v):
        return 4.0 * v - shift(v, 1, 0) - shift(v, -1, 0) - shift(v, 1, 1) - shift(v, -1, 1)

    twice = laplace(jnp.where(inside, laplace(wide), 0.0))[rows:2 * rows, 128:128 + half]

    base = REG * twice + base
    to_cp.wait_send()

    @pl.when(has_c)
    def _():
        to_cc.wait_send()

    to_ps.wait_send()
    to_ps.wait_recv()
    hess[...] = base + scale * pr[...]


def store(image_v, hess_v, image_h, hess_h, sem):
    copies = [
        pltpu.make_async_copy(image_v.at[c, z], image_h.at[c, z], sem.at[2 * c + z])
        for c in range(3)
        for z in range(2)
    ]
    copies.append(pltpu.make_async_copy(hess_v, hess_h, sem.at[6]))
    for copy in copies:
        copy.start()
    for copy in copies:
        copy.wait()


def local(sizes, velocity, adjoint, viscosity, hang_flags, hang_index, block_table, friction, basal_mask, direction):
    _, levels, rows, cols = velocity.shape
    assert levels == 2 and sizes[2] == 2 and cols == 384
    half = direction.shape[1]
    f32 = jnp.float32
    vmem = pltpu.VMEM
    anywhere = pl.BlockSpec(memory_space=pltpu.HBM)
    arguments = [
        pltpu.with_memory_space_constraint(array, pltpu.HBM)
        for array in (
            velocity, adjoint, viscosity, hang_flags, hang_index,
            jnp.transpose(block_table, (1, 2, 0)), friction, basal_mask, direction,
        )
    ]
    image, hess = pl.pallas_call(
        functools.partial(kernel, sizes),
        out_shape=(vmem(velocity.shape, f32), vmem(direction.shape, f32)),
        in_specs=[anywhere] * 9,
        out_specs=(pl.BlockSpec(memory_space=vmem),) * 2,
        scratch_shapes=[
            pltpu.SMEM((3, 3, NB), f32),
            vmem(velocity.shape, f32),
            vmem(velocity.shape, f32),
            vmem(hang_flags.shape, jnp.int32),
            vmem(hang_index.shape, jnp.int32),
            vmem(direction.shape, f32),
            vmem(direction.shape, jnp.int32),
            vmem(direction.shape, f32),
            vmem((levels, 4, rows, cols), f32),
            vmem((8, cols + 128), f32),
            vmem((8, cols + 128), f32),
            vmem((8, cols + 128), f32),
            vmem((8, cols + 128), f32),
            vmem((4, rows, cols), f32),
            vmem((levels, 4, rows, 128), f32),
            vmem((levels, 4, rows, 128), f32),
            vmem((3 * rows, 384), f32),
            vmem((3 * rows, 128), f32),
            vmem((3 * rows, 128), f32),
            vmem((3 * rows, 128), f32),
            vmem((3 * rows, 128), f32),
            vmem(direction.shape, f32),
            vmem(direction.shape, f32),
            pltpu.SemaphoreType.DMA((9,)),
            pltpu.SemaphoreType.DMA((11,)),
            pltpu.SemaphoreType.DMA((11,)),
        ],
        compiler_params=pltpu.CompilerParams(collective_id=0, has_side_effects=True, vmem_limit_bytes=LIMIT),
        cost_estimate=pl.CostEstimate(flops=200_000, bytes_accessed=400_000, transcendentals=1536),
        name="hessian_apply",
    )(*arguments)
    return pl.pallas_call(
        store,
        out_shape=(
            jax.ShapeDtypeStruct(velocity.shape, f32),
            jax.ShapeDtypeStruct(direction.shape, f32),
        ),
        in_specs=[pl.BlockSpec(memory_space=vmem)] * 2,
        out_specs=(anywhere,) * 2,
        scratch_shapes=[pltpu.SemaphoreType.DMA((7,))],
        compiler_params=pltpu.CompilerParams(vmem_limit_bytes=LIMIT),
        name="store",
    )(image, hess)


def solution(mesh):
    sizes = tuple(mesh.shape[axis] for axis in ("gx", "gy", "gz"))
    return jax.shard_map(
        functools.partial(local, sizes),
        mesh=mesh,
        in_specs=(
            P(None, "gz", "gx", "gy"),
            P(None, "gz", "gx", "gy"),
            P("gz", "gx", "gy"),
            P("gx", "gy"),
            P("gx", "gy"),
            P(),
            P("gx", ("gy", "gz")),
            P("gx", ("gy", "gz")),
            P("gx", ("gy", "gz")),
        ),
        out_specs=(P(None, "gz", "gx", "gy"), P("gx", ("gy", "gz"))),
        check_vma=False,
    )
```

```python
import functools

import jax
import jax.numpy as jnp
from jax import lax
from jax.experimental import pallas as pl
from jax.experimental.pallas import tpu as pltpu
from jax.sharding import PartitionSpec as P

NB = 8
REG = 0.05
LIMIT = 4 * 1024 * 1024
MESH = pl.DeviceIdType.MESH
XU, XD, YL, YR, ZZ, CP, CC, PS = range(8)


def shift(value, by, axis):
    return pltpu.roll(value, by % value.shape[axis], axis)


def kernel(
    sizes,
    vel_h, adj_h, visc_h, flags_h, index_h, table_h, fric_h, mask_h, dir_h,
    out, hess,
    table, vel, adj, flags, index, fric, mask, direc,
    cons, xs_u, xs_d, xr_u, xr_d, zr, yr_l, yr_r, big, cs_p, cs_c, cr_p, cr_c, ps, pr,
    load_sem, send_sem, recv_sem,
):
    ngx, ngy, ngz = sizes
    gx, gy, gz = (lax.axis_index(axis) for axis in ("gx", "gy", "gz"))
    rows, cols = cons.shape[2], cons.shape[3]
    tiles = [slice(128 * m, 128 * (m + 1)) for m in range(3)]
    half = direc.shape[1]
    low = gz == 0
    has_u, has_d = gx > 0, gx < ngx - 1
    has_l, has_r = gy > 0, gy < ngy - 1
    has_c = jnp.where(low, gy, ngy - 1 - gy) > 0
    cross_gy = jnp.where(low, gy + ngy - 1, gy + 1) % ngy

    loads = [
        pltpu.make_async_copy(src, dst, load_sem.at[i])
        for i, (src, dst) in enumerate(
            (
                (table_h, table), (flags_h, flags), (index_h, index), (vel_h, vel), (visc_h, cons.at[:, 3]),
                (dir_h, direc), (adj_h, adj), (fric_h, fric), (mask_h, mask),
            )
        )
    ]

    up = {"gx": (gx + ngx - 1) % ngx}
    down = {"gx": (gx + 1) % ngx}
    left = {"gy": (gy + ngy - 1) % ngy}
    right = {"gy": (gy + 1) % ngy}
    partner = {"gz": 1 - gz}
    cross = {"gy": cross_gy, "gz": 1 - gz}
    greet = ((has_u, up), (has_d, down), (has_l, left), (has_r, right), (has_c, cross))

    barrier = pltpu.get_barrier_semaphore()
    pl.semaphore_signal(barrier, inc=1, device_id=partner, device_id_type=MESH)
    for has, device in greet:
        @pl.when(has)
        def _():
            pl.semaphore_signal(barrier, inc=1, device_id=device, device_id_type=MESH)

    for load in loads:
        load.start()

    big[...] = jnp.zeros_like(big)
    for has, buffers in (
        (has_u, (xr_u,)), (has_d, (xr_d,)), (has_l, (yr_l,)), (has_r, (yr_r,)), (has_c, (cr_c,))
    ):
        @pl.when(jnp.logical_not(has))
        def _():
            for buffer in buffers:
                buffer[...] = jnp.zeros_like(buffer)

    def remote(src, dst, at, device):
        return pltpu.make_async_remote_copy(
            src_ref=src, dst_ref=dst, send_sem=send_sem.at[at], recv_sem=recv_sem.at[at],
            device_id=device, device_id_type=MESH,
        )

    to_xu = remote(xs_d, xr_u, XU, down)
    to_xd = remote(xs_u, xr_d, XD, up)
    to_yl = remote(cons.at[:, :, :, cols - 128:], yr_l, YL, right)
    to_yr = remote(cons.at[:, :, :, :128], yr_r, YR, left)
    near, far = 1 - gz, gz
    to_z = remote(cons.at[near], zr, ZZ, partner)
    to_cp = remote(cs_p, cr_p, CP, partner)
    to_cc = remote(cs_c, cr_c, CC, cross)
    to_ps = remote(ps, pr, PS, partner)

    for load in loads[:6]:
        load.wait()
    hanging = flags[...] == 1
    number = index[...]
    chosen = [number == n for n in range(NB)]
    block = [[None] * 3 for _ in range(3)]
    for m in range(3):
        for k in range(3):
            value = jnp.full(number.shape, table[m, k, 0], jnp.float32)
            for n in range(1, NB):
                value = jnp.where(chosen[n], table[m, k, n], value)
            block[m][k] = jnp.where(hanging, value, 1.0 if m == k else 0.0)
    for z in range(2):
        for c in range(3):
            slots = [vel[c, z, :, tile] for tile in tiles]
            for m in range(3):
                cons[z, c, :, tiles[m]] = (
                    block[m][0] * slots[0] + block[m][1] * slots[1] + block[m][2] * slots[2]
                )
    for i, z in enumerate((near, far)):
        for c in range(4):
            at = 4 * i + c
            xs_u[at:at + 1, :cols] = cons[z, c, 0:1, :]
            xs_d[at:at + 1, :cols] = cons[z, c, rows - 1:rows, :]
    for r in range(2):
        for send, row in ((xs_u, r), (xs_d, rows - 2 + r)):
            send[2 * r:2 * r + 1, cols:cols + 128] = direc[row:row + 1, :128]
            send[2 * r + 1:2 * r + 2, cols:cols + half - 128] = direc[row:row + 1, 128:]

    big[rows:2 * rows, 128:128 + half] = direc[...]
    waits = sum((has.astype(jnp.int32) for has, _ in greet), jnp.int32(1))
    pl.semaphore_wait(barrier, waits)
    for has, copy in ((has_d, to_xu), (has_u, to_xd)):
        @pl.when(has)
        def _():
            copy.start()
    to_z.start()
    for has, copy in ((has_r, to_yl), (has_l, to_yr)):
        @pl.when(has)
        def _():
            copy.start()

    row_at = lax.broadcasted_iota(jnp.int32, (rows, cols), 0)
    lane_at = lax.broadcasted_iota(jnp.int32, (rows, cols), 1)
    inner_row, inner_lane = row_at < rows - 1, lane_at < cols - 1
    own = [[cons[z, c] for c in range(4)] for z in (near, far)]
    total = [[None] * 3 for _ in range(2)]
    visc_z = own[0][3] + own[1][3]
    for c in range(3):
        flux = visc_z * (own[0][c] - own[1][c])
        total[0][c] = flux
        total[1][c] = own[1][3] * own[1][c] - flux
    for i in range(2):
        for axis, inner in ((0, inner_row), (1, inner_lane)):
            visc = own[i][3]
            visc = jnp.where(inner, visc + shift(visc, -1, axis), 0.0)
            for c in range(3):
                a = own[i][c]
                flux = visc * (a - shift(a, -1, axis))
                total[i][c] = total[i][c] + flux - shift(flux, 1, axis)

    for has, copy in ((has_u, to_xu), (has_d, to_xd)):
        @pl.when(has)
        def _():
            copy.wait_recv()
    for buffer, row in ((xr_u, rows - 2), (xr_d, 2 * rows)):
        for r in range(2):
            big[row + r:row + r + 1, 128:256] = buffer[2 * r:2 * r + 1, cols:cols + 128]
            big[row + r:row + r + 1, 256:128 + half] = (
                buffer[2 * r + 1:2 * r + 2, cols:cols + half - 128]
            )
    wide = big[...]
    edge_low, edge_high = wide[:, 128:256], wide[:, half:half + 128]
    cs_p[...] = jnp.where(low, edge_high, edge_low)
    cs_c[...] = jnp.where(low, edge_low, edge_high)
    to_cp.start()

    @pl.when(has_c)
    def _():
        to_cc.start()

    for sent, got, row in ((xs_u, xr_u, 0), (xs_d, xr_d, rows - 1)):
        mine, other = sent[:, :cols], got[:, :cols]
        gap, visc = mine - other, mine + other
        for i in range(2):
            for c in range(3):
                flux = visc[4 * i + 3:4 * i + 4] * gap[4 * i + c:4 * i + c + 1]
                total[i][c] = total[i][c] + jnp.where(row_at == row, flux, 0.0)
    for has, copy in ((has_l, to_yl), (has_r, to_yr)):
        @pl.when(has)
        def _():
            copy.wait_recv()
    total = [[[total[i][c][:, tile] for tile in tiles] for c in range(3)] for i in range(2)]
    lane = lax.broadcasted_iota(jnp.int32, (rows, 128), 1)
    for got, by, at, m in ((yr_l, 1, 0, 0), (yr_r, -1, 127, 2)):
        for i, z in enumerate((near, far)):
            visc = own[i][3][:, tiles[m]] + shift(got[z, 3], by, 1)
            visc = jnp.where(lane == at, visc, 0.0)
            for c in range(3):
                gap = own[i][c][:, tiles[m]] - shift(got[z, c], by, 1)
                total[i][c][m] = total[i][c][m] + visc * gap

    for load in loads[6:]:
        load.wait()
    sums = [None] * 3

    def finish(applied, c, z):
        applied = [0.5 * a for a in applied]
        for k in range(3):
            image = block[0][k] * applied[0] + block[1][k] * applied[1] + block[2][k] * applied[2]
            out[c, z, :, tiles[k]] = image
            term = image * adj[c, z, :, tiles[k]]
            sums[k] = term if sums[k] is None else sums[k] + term

    for c in range(3):
        finish(total[1][c], c, far)
    to_z.wait_recv()
    visc_z = own[0][3] + zr[3]
    for c in range(3):
        flux = visc_z * (own[0][c] - zr[c])
        finish([total[0][c][m] + flux[:, tiles[m]] for m in range(3)], c, near)
    sums = jnp.concatenate(sums, axis=1)
    first, second = sums[:, :half], sums[:, half:]
    ps[...] = jnp.where(low, second, first)
    to_ps.start()
    mine = jnp.where(low, first, second)

    scale = mask[...].astype(jnp.float32) * jnp.exp(fric[...])
    row_g = gx * rows - rows + lax.broadcasted_iota(jnp.int32, wide.shape, 0)
    col_g = (gy * ngz + gz) * half - 128 + lax.broadcasted_iota(jnp.int32, wide.shape, 1)
    inside = (row_g >= 0) & (row_g < ngx * rows) & (col_g >= 0) & (col_g < ngy * ngz * half)
    base = scale * mine
    to_z.wait_send()
    for has, copy in ((has_d, to_xu), (has_u, to_xd), (has_r, to_yl), (has_l, to_yr)):
        @pl.when(has)
        def _():
            copy.wait_send()
    to_cp.wait_recv()

    @pl.when(has_c)
    def _():
        to_cc.wait_recv()

    from_p, from_c = cr_p[...], cr_c[...]
    from_low = jnp.where(low, from_c, from_p)
    from_high = shift(jnp.where(low, from_p, from_c), half % 128, 1)
    lane = lax.broadcasted_iota(jnp.int32, from_low.shape, 1)
    wide = jnp.concatenate(
        [from_low, wide[:, 128:256], jnp.where(lane < half % 128, wide[:, 256:], from_high)], axis=1
    )

    def laplace(v):
        return 4.0 * v - shift(v, 1, 0) - shift(v, -1, 0) - shift(v, 1, 1) - shift(v, -1, 1)

    twice = laplace(jnp.where(inside, laplace(wide), 0.0))[rows:2 * rows, 128:128 + half]

    base = REG * twice + base
    to_cp.wait_send()

    @pl.when(has_c)
    def _():
        to_cc.wait_send()

    to_ps.wait_send()
    to_ps.wait_recv()
    hess[...] = base + scale * pr[...]


def store(image_v, hess_v, image_h, hess_h, sem):
    copies = [
        pltpu.make_async_copy(image_v, image_h, sem.at[0]),
        pltpu.make_async_copy(hess_v, hess_h, sem.at[1]),
    ]
    for copy in copies:
        copy.start()
    for copy in copies:
        copy.wait()


def local(sizes, velocity, adjoint, viscosity, hang_flags, hang_index, block_table, friction, basal_mask, direction):
    _, levels, rows, cols = velocity.shape
    assert levels == 2 and sizes[2] == 2 and cols == 384
    half = direction.shape[1]
    f32 = jnp.float32
    vmem = pltpu.VMEM
    anywhere = pl.BlockSpec(memory_space=pltpu.HBM)
    arguments = [
        pltpu.with_memory_space_constraint(array, pltpu.HBM)
        for array in (
            velocity, adjoint, viscosity, hang_flags, hang_index,
            jnp.transpose(block_table, (1, 2, 0)), friction, basal_mask, direction,
        )
    ]
    image, hess = pl.pallas_call(
        functools.partial(kernel, sizes),
        out_shape=(vmem(velocity.shape, f32), vmem(direction.shape, f32)),
        in_specs=[anywhere] * 9,
        out_specs=(pl.BlockSpec(memory_space=vmem),) * 2,
        scratch_shapes=[
            pltpu.SMEM((3, 3, NB), f32),
            vmem(velocity.shape, f32),
            vmem(velocity.shape, f32),
            vmem(hang_flags.shape, jnp.int32),
            vmem(hang_index.shape, jnp.int32),
            vmem(direction.shape, f32),
            vmem(direction.shape, jnp.int32),
            vmem(direction.shape, f32),
            vmem((levels, 4, rows, cols), f32),
            vmem((8, cols + 128), f32),
            vmem((8, cols + 128), f32),
            vmem((8, cols + 128), f32),
            vmem((8, cols + 128), f32),
            vmem((4, rows, cols), f32),
            vmem((levels, 4, rows, 128), f32),
            vmem((levels, 4, rows, 128), f32),
            vmem((3 * rows, 384), f32),
            vmem((3 * rows, 128), f32),
            vmem((3 * rows, 128), f32),
            vmem((3 * rows, 128), f32),
            vmem((3 * rows, 128), f32),
            vmem(direction.shape, f32),
            vmem(direction.shape, f32),
            pltpu.SemaphoreType.DMA((9,)),
            pltpu.SemaphoreType.DMA((8,)),
            pltpu.SemaphoreType.DMA((8,)),
        ],
        compiler_params=pltpu.CompilerParams(collective_id=0, has_side_effects=True, vmem_limit_bytes=LIMIT),
        cost_estimate=pl.CostEstimate(flops=200_000, bytes_accessed=400_000, transcendentals=1536),
        name="hessian_apply",
    )(*arguments)
    return pl.pallas_call(
        store,
        out_shape=(
            jax.ShapeDtypeStruct(velocity.shape, f32),
            jax.ShapeDtypeStruct(direction.shape, f32),
        ),
        in_specs=[pl.BlockSpec(memory_space=vmem)] * 2,
        out_specs=(anywhere,) * 2,
        scratch_shapes=[pltpu.SemaphoreType.DMA((2,))],
        compiler_params=pltpu.CompilerParams(vmem_limit_bytes=LIMIT),
        name="store",
    )(image, hess)


def solution(mesh):
    sizes = tuple(mesh.shape[axis] for axis in ("gx", "gy", "gz"))
    return jax.shard_map(
        functools.partial(local, sizes),
        mesh=mesh,
        in_specs=(
            P(None, "gz", "gx", "gy"),
            P(None, "gz", "gx", "gy"),
            P("gz", "gx", "gy"),
            P("gx", "gy"),
            P("gx", "gy"),
            P(),
            P("gx", ("gy", "gz")),
            P("gx", ("gy", "gz")),
            P("gx", ("gy", "gz")),
        ),
        out_specs=(P(None, "gz", "gx", "gy"), P("gx", ("gy", "gz"))),
        check_vma=False,
    )
```
